128 devices in a mesh: blk: 32 (over x, z, y_lo), pre: 4 (over y_hi, core).
Axes of the slice: x: 4, y: 4 (y_hi: 2, y_lo: 2; y = y_hi * 2 + y_lo), z: 4, core: 2. Of those that a mesh axis runs over, the one named last changes fastest.
Arguments:
- record: bfloat16 [4096, 131072], P('blk', 'pre'), may hold values from -6 to 6
- quality: int32 [4096], P('blk'), may hold values 0 or 1
Outputs:
- stacks: float32 [4, 4, 64, 4096, 128], P('pre', None, None, 'blk')
The draws below stay inside these ranges and needn't reach their ends.
All inputs are finite; a program needn't handle non-finite values. No bound on the sum of `quality` on one device may be relied on, other than what follows from the above.
Results may differ from the reference program's by a relative error of at most 0.0048.
Values may be sent and summed in bfloat16 or wider, within the bound.
A program may use at most 128 MiB of HBM per device.

```python
import math
import jax
import jax.numpy as jnp
from jax import lax

CB = 128
NFR = 16
M = 512
R = 4
KT = 16
FB = 128
NLAG = 64
PAIRS = 4
FR = 32
BAND0 = 16
NT = 131072
NCH = 4096
NSEG = 4
N_BLK = 32


def place_ends(array, own_key, low, top_value):
    index_at = [jax.random.randint(jax.random.fold_in(own_key, axis), (), 0, length) for axis, length in enumerate(array.shape)]
    longest = array.shape.index(max(array.shape))
    next_to = index_at[:longest] + [(index_at[longest] + 1) % array.shape[longest]] + index_at[longest + 1:]
    return array.at[tuple(index_at)].set(low).at[tuple(next_to)].set(top_value)


def levels(rng, shape, split, smallest, high):
    loudness = 1.0
    for position, parts in split:
        draws = jax.random.uniform(jax.random.fold_in(jax.random.fold_in(rng, 6), position), (parts,), jnp.float32, smallest / len(split), high / len(split))
        loudness = loudness * jnp.repeat(jnp.exp(draws), shape[position] // parts).reshape((-1,) + (1,) * (len(shape) - 1 - position))
    return loudness


def centred(rng, shape, deviation, most, shards=(), held_as=jnp.bfloat16):
    array = jax.random.normal(rng, shape, jnp.float32) * deviation
    if len(shards) > 0:
        array = levels(rng, shape, shards, -0.22, 0.18) * array
    return jnp.clip(array, min=-most, max=most).astype(held_as)


def setup_inputs(seed: int = 0) -> dict:
    streams_of = jax.random.split(jax.random.key(seed), 3)
    return {
        "record": centred(streams_of[0], (NCH, NT), 1.0, 6.0, ((0, 32), (1, 4))),
        "quality": place_ends((jax.random.randint(streams_of[1], (NCH,), 0, 8) < 7).astype(jnp.int32), jax.random.fold_in(streams_of[1], 1), 0, 1),
    }


def filter_taps():
    index = jnp.arange(KT, dtype=jnp.int32).astype(jnp.float32)
    centre = (KT - 1) / 2.0
    shaped = jnp.sinc((index - centre) / R) * (0.54 - 0.46 * jnp.cos(2.0 * math.pi * index / (KT - 1)))
    return (shaped / jnp.sum(shaped)).astype(jnp.bfloat16)

def dft_table():
    sample = jnp.arange(M, dtype=jnp.int32)
    bins = BAND0 + jnp.arange(FB, dtype=jnp.int32)
    phase = (sample[:, None] * bins[None, :] % M).astype(jnp.float32)
    angle = 2.0 * math.pi * phase / M
    hann = 0.5 - 0.5 * jnp.cos(2.0 * math.pi * sample.astype(jnp.float32) / M)
    return jnp.concatenate([hann[:, None] * jnp.cos(angle), -hann[:, None] * jnp.sin(angle)], 1)

def lag_table():
    bins = BAND0 + jnp.arange(FB, dtype=jnp.int32)
    lags = jnp.arange(NLAG, dtype=jnp.int32) - NLAG // 2
    phase = (bins[:, None] * (lags[None, :] + M) % M).astype(jnp.float32)
    angle = 2.0 * math.pi * phase / M
    return jnp.concatenate([jnp.cos(angle), -jnp.sin(angle)], 0).astype(jnp.bfloat16)

def whiten(spec, quality):
    real_part = spec[..., :FB]
    imag_part = spec[..., FB:]
    power = real_part * real_part + imag_part * imag_part
    level = lax.optimization_barrier(jnp.mean(power, axis=-1, keepdims=True))
    amp = jnp.sqrt(power + 0.1 * level + 1e-06)
    keep = quality.astype(jnp.float32)[:, None, None]
    return (jnp.concatenate([real_part / amp, imag_part / amp], -1) * keep).astype(jnp.bfloat16)

def block_spectra(block, quality):
    padding = jnp.zeros((CB, R * M), jnp.bfloat16)
    extended = jnp.concatenate([block, padding], 1).astype(jnp.float32)
    grouped = extended.reshape(CB, (NT + R * M) // R, R)
    count = NSEG * NFR * M + M // 2
    weights = filter_taps().astype(jnp.float32).reshape(KT // R, R)
    decimated = jnp.zeros((CB, count), jnp.float32)
    for offset in range(KT // R):
        decimated = decimated + jnp.einsum('cmr,r->cm', grouped[:, offset:offset + count], weights[offset])
    halves = decimated.reshape(CB, 2 * NSEG * NFR + 1, M // 2)
    frames = jnp.concatenate([halves[:, :-1], halves[:, 1:]], 2)
    spec = jnp.einsum('csm,mg->csg', frames, dft_table(), precision=lax.Precision.HIGHEST)
    return whiten(spec, quality)

def correlate(own, other, table):
    own_f = own.astype(jnp.float32)
    other_f = other.astype(jnp.float32)
    own_re, own_im = (own_f[..., :FB], own_f[..., FB:])
    other_re, other_im = (other_f[..., :FB], other_f[..., FB:])
    cross_re = jnp.einsum('csf,dsf->fcd', own_re, other_re) + jnp.einsum('csf,dsf->fcd', own_im, other_im)
    cross_im = jnp.einsum('csf,dsf->fcd', own_im, other_re) - jnp.einsum('csf,dsf->fcd', own_re, other_im)
    joined = jnp.concatenate([cross_re.astype(jnp.bfloat16), cross_im.astype(jnp.bfloat16)], 0).astype(jnp.float32)
    return jnp.einsum('gcd,gl->lcd', joined, table.astype(jnp.float32)) * (FR * FB) ** (-0.5)

def reference(record, quality):
    blocks = record.reshape(N_BLK, CB, NT)
    masks = quality.reshape(N_BLK, CB)
    whitened = lax.map(lambda pair: block_spectra(pair[0], pair[1]), (blocks, masks))
    table = lag_table()
    zero = jnp.int32(0)

    def one_item(item):
        segment = (item // N_BLK).astype(jnp.int32)
        block_id = (item % N_BLK).astype(jnp.int32)
        start = (segment * FR).astype(jnp.int32)
        own = lax.dynamic_slice(whitened, (block_id, zero, start, zero), (1, CB, FR, 2 * FB))[0]
        results = []
        for offset in range(PAIRS):
            partner = ((block_id - offset + N_BLK) % N_BLK).astype(jnp.int32)
            other = lax.dynamic_slice(whitened, (partner, zero, start, zero), (1, CB, FR, 2 * FB))[0]
            results.append(correlate(own, other, table))
        return jnp.stack(results, 0)
    items = jnp.arange(NSEG * N_BLK, dtype=jnp.int32)
    stacked = lax.map(one_item, items)
    stacked = stacked.reshape(NSEG, N_BLK, PAIRS, NLAG, CB, CB)
    return jnp.transpose(stacked, (0, 2, 3, 1, 4, 5)).reshape(NSEG, PAIRS, NLAG, NCH, CB)
```

```python
import math

import jax
import jax.numpy as jnp
import ml_dtypes
import numpy as np
from jax import lax
from jax.experimental import pallas as pl
from jax.experimental.pallas import tpu as pltpu
from jax.sharding import PartitionSpec as P

M = 512
R = 4
KT = 16
FB = 128
NLAG = 64
BAND0 = 16
CH = 128
HALF = 1024
FRAMES = 32
GROUPS = 32
ROWS = (GROUPS + 2) * 8
HALO = HALF + 128
NT = (((1,), (1,)), ((), ()))
BF = jnp.bfloat16
F32 = jnp.float32


def filter_taps():
    index = np.arange(KT, dtype=np.float32)
    centre = np.float32((KT - 1) / 2.0)
    shaped = np.sinc((index - centre) / np.float32(R)) * (
        0.54 - 0.46 * np.cos(2.0 * math.pi * index / (KT - 1))
    )
    return (shaped / np.sum(shaped)).astype(np.float32).astype(ml_dtypes.bfloat16)


def split(table):
    high = table.astype(np.float32).astype(ml_dtypes.bfloat16)
    low = (table - high.astype(np.float64)).astype(np.float32).astype(ml_dtypes.bfloat16)
    return high, low


def half_tables():
    taps = filter_taps().astype(np.float64)
    toeplitz = np.zeros((M // 2, HALF + 128))
    for m in range(M // 2):
        toeplitz[m, R * m : R * m + KT] = taps
    group = np.arange(-1, GROUPS + 1)
    bins = BAND0 + group[:, None] + 32 * np.arange(4)[None, :]
    phase = 2.0 * math.pi * ((bins[:, :, None] * np.arange(M // 2)) % M) / M
    both = np.stack([np.cos(phase), -np.sin(phase)], 1).reshape(ROWS, M // 2)
    table = both @ toeplitz
    high, low = split(table)
    main = np.concatenate([high[:, :HALF], low[:, :HALF]], 0)
    tail = np.concatenate([high[:, HALF:], low[:, HALF:]], 1)
    return main, tail


def lag_table():
    lags = np.arange(NLAG) - NLAG // 2
    bins = (BAND0 + np.arange(GROUPS)[:, None, None] + 32 * np.arange(4)[None, None, :])
    phase = 2.0 * math.pi * (((lags[:, None, None, None] + M) * bins[None]) % M) / M
    both = np.concatenate([np.cos(phase), -np.sin(phase)], 2).reshape(NLAG, 2 * FB)
    rounded = both.astype(np.float32).astype(ml_dtypes.bfloat16).astype(np.float32)
    return (rounded / 64.0).astype(ml_dtypes.bfloat16)


def spread_table():
    table = np.zeros((CH, 2, 4, 2, CH), np.float32)
    for c in range(CH):
        for o in range(2):
            table[c, o, :, o, c] = 1.0
    return table.reshape(CH * 8, 2 * CH).astype(ml_dtypes.bfloat16)


def spectra_kernel(main_ref, tail_ref, quality_ref, first_ref, one_ref, two_ref, three_ref, halo_ref,
                   white_ref, turned_ref, held):
    step = pl.program_id(0)
    last = step == FRAMES // 2 - 1

    def transform(raw, after):
        both = lax.dot_general(main_ref[...], raw, NT, preferred_element_type=F32)
        ends = jnp.concatenate([after, after], 1)
        return (both[:ROWS] + both[ROWS:]) + lax.dot_general(
            tail_ref[...], ends, NT, preferred_element_type=F32)

    @pl.when(step == 0)
    def _():
        held[...] = transform(first_ref[...], one_ref[:, :128]).reshape(GROUPS + 2, 8, CH)

    two = jnp.where(last, halo_ref[:, :HALF], two_ref[...])
    three = jnp.where(last, halo_ref[:, HALF:], three_ref[...])
    raw = jnp.concatenate([one_ref[...], two], 0)
    after = jnp.concatenate([two[:, :128], three], 0)
    pair = transform(raw, after)
    zero = held[...]
    first = pair[:, :CH].reshape(GROUPS + 2, 8, CH)
    second = pair[:, CH:].reshape(GROUPS + 2, 8, CH)
    held[...] = second
    group = lax.broadcasted_iota(jnp.int32, (GROUPS, 8, CH), 0)
    odd = (group % 2) == 1
    row = lax.broadcasted_iota(jnp.int32, (GROUPS, 8, CH), 1)
    keep = quality_ref[...].reshape(1, 1, CH)

    def whiten(front, back):
        side = 0.25 * (front[:GROUPS] + front[2:])
        spec = 0.5 * front[1 : GROUPS + 1] - side
        other = 0.5 * back[1 : GROUPS + 1] + 0.25 * (back[:GROUPS] + back[2:])
        spec = spec + jnp.where(odd, -other, other)
        square = spec * spec
        level = jnp.sum(jnp.sum(square, 0), 0, keepdims=True).reshape(1, 1, CH) * (1.0 / FB)
        power = square + pltpu.roll(square, 4, 1)
        white = spec * lax.rsqrt(power + (0.1 * level + 1e-06)) * keep
        turned = pltpu.roll(white, 4, 1)
        return white, jnp.where(row < 4, turned, -turned)

    w0, t0 = whiten(zero, first)
    w1, t1 = whiten(first, second)
    white_ref[...] = jnp.concatenate([w0, w1], 1).astype(BF)
    turned_ref[...] = jnp.concatenate([t0, t1], 1).astype(BF)


def spectra(record, halo, quality):
    main, tail = half_tables()
    keep = quality.astype(F32).reshape(1, CH)
    whole = lambda *shape: pl.BlockSpec(shape, lambda i: (0,) * len(shape))
    out = jax.ShapeDtypeStruct((GROUPS, FRAMES * 8, CH), BF)
    return pl.pallas_call(
        spectra_kernel,
        grid=(FRAMES // 2,),
        out_shape=(out, out),
        in_specs=[
            whole(2 * ROWS, HALF),
            whole(ROWS, 256),
            whole(1, CH),
            pl.BlockSpec((CH, HALF), lambda i: (0, 0)),
            pl.BlockSpec((CH, HALF), lambda i: (0, 2 * i + 1)),
            pl.BlockSpec((CH, HALF), lambda i: (0, jnp.minimum(2 * i + 2, FRAMES - 1))),
            pl.BlockSpec((CH, 128), lambda i: (0, jnp.minimum((2 * i + 3) * 8, FRAMES * 8 - 1))),
            whole(CH, HALO),
        ],
        out_specs=[pl.BlockSpec((GROUPS, 16, CH), lambda i: (0, i, 0))] * 2,
        scratch_shapes=[pltpu.VMEM((GROUPS + 2, 8, CH), F32)],
        compiler_params=pltpu.CompilerParams(vmem_limit_bytes=40 * 2**20),
        name="spectra",
    )(jnp.asarray(main), jnp.asarray(tail), keep, record, record, record, record, halo)


CBLK = 32


def correlate_kernel(spread_ref, lag_ref, white_ref, turned_ref, p1_ref, p2_ref, p3_ref, out_ref, cross):
    rows = lax.broadcasted_iota(jnp.int32, (CBLK * 8, 256), 0)
    cols = lax.broadcasted_iota(jnp.int32, (CBLK * 8, 256), 1)
    diagonal = (rows % 4) == (cols % 4)

    def stage(group):
        own = jnp.concatenate([white_ref[group], turned_ref[group]], 1)
        left = lax.dot_general(spread_ref[...], own, NT, preferred_element_type=F32)
        left = jnp.where(diagonal, left, 0.0).astype(BF)
        right = jnp.concatenate([white_ref[group], p1_ref[group], p2_ref[group], p3_ref[group]], 1)
        return jnp.dot(left, right, preferred_element_type=F32).reshape(CBLK, 8, 4 * CH)

    @pl.loop(0, GROUPS // 2)
    def _(pair):
        both = jnp.concatenate([stage(2 * pair), stage(2 * pair + 1)], 1)
        cross[:, pl.ds(pl.multiple_of(pair * 16, 16), 16), :] = both.astype(BF)

    @pl.loop(0, CBLK)
    def _(c):
        result = jnp.dot(lag_ref[...], cross[c], preferred_element_type=F32)
        for d in range(4):
            flat = out_ref.at[d].reshape(NLAG * CBLK, CH)
            flat[pl.ds(c, NLAG, stride=CBLK), :] = result[:, d * CH : (d + 1) * CH]


def correlate(white, turned, partners):
    whole = lambda *shape: pl.BlockSpec(shape, lambda i: (0,) * len(shape))
    spectrum = whole(GROUPS, 256, CH)
    return pl.pallas_call(
        correlate_kernel,
        grid=(CH // CBLK,),
        out_shape=jax.ShapeDtypeStruct((4, NLAG, CH, CH), F32),
        in_specs=[pl.BlockSpec((CBLK * 8, 256), lambda i: (i, 0)), whole(NLAG, 256)] + [spectrum] * 5,
        out_specs=pl.BlockSpec((4, NLAG, CBLK, CH), lambda i: (0, 0, i, 0)),
        scratch_shapes=[pltpu.VMEM((CBLK, 256, 4 * CH), BF)],
        compiler_params=pltpu.CompilerParams(vmem_limit_bytes=60 * 2**20),
        name="correlate",
    )(jnp.asarray(spread_table()), jnp.asarray(lag_table()), white, turned, *partners)


def shards(record, quality):
    count = lax.axis_size("pre")
    halo = lax.ppermute(record[:, :HALO], "pre", [(i, i - 1) for i in range(1, count)])
    white, turned = spectra(record, halo, quality)
    blocks = lax.axis_size("blk")
    partners = [
        lax.ppermute(white, "blk", [(i, (i + d) % blocks) for i in range(blocks)]) for d in range(1, 4)
    ]
    return correlate(white, turned, partners)[None]


def solution(mesh):
    placed = (P("blk", "pre"), P("blk"))
    return jax.shard_map(
        shards,
        mesh=mesh,
        in_specs=placed,
        out_specs=P("pre", None, None, "blk", None),
        check_vma=False,
    )
```

```python
import math

import jax
import jax.numpy as jnp
import ml_dtypes
import numpy as np
from jax import lax
from jax.experimental import pallas as pl
from jax.experimental.pallas import tpu as pltpu
from jax.sharding import PartitionSpec as P

M = 512
R = 4
KT = 16
FB = 128
NLAG = 64
BAND0 = 16
CH = 128
HALF = 1024
FRAMES = 32
GROUPS = 32
ROWS = (GROUPS + 2) * 8
HALO = HALF + 128
NT = (((1,), (1,)), ((), ()))
BF = jnp.bfloat16
F32 = jnp.float32


def filter_taps():
    index = np.arange(KT, dtype=np.float32)
    centre = np.float32((KT - 1) / 2.0)
    shaped = np.sinc((index - centre) / np.float32(R)) * (
        0.54 - 0.46 * np.cos(2.0 * math.pi * index / (KT - 1))
    )
    return (shaped / np.sum(shaped)).astype(np.float32).astype(ml_dtypes.bfloat16)


def split(table):
    high = table.astype(np.float32).astype(ml_dtypes.bfloat16)
    low = (table - high.astype(np.float64)).astype(np.float32).astype(ml_dtypes.bfloat16)
    return high, low


def half_tables():
    taps = filter_taps().astype(np.float64)
    toeplitz = np.zeros((M // 2, HALF + 128))
    for m in range(M // 2):
        toeplitz[m, R * m : R * m + KT] = taps
    group = np.arange(-1, GROUPS + 1)
    bins = BAND0 + group[:, None] + 32 * np.arange(4)[None, :]
    phase = 2.0 * math.pi * ((bins[:, :, None] * np.arange(M // 2)) % M) / M
    both = np.stack([np.cos(phase), -np.sin(phase)], 1).reshape(ROWS, M // 2)
    table = both @ toeplitz
    high, low = split(table)
    main = np.concatenate([high[:, :HALF], low[:, :HALF]], 0)
    tail = np.concatenate([high[:, HALF:], low[:, HALF:]], 1)
    return main, tail


def lag_table():
    lags = np.arange(NLAG) - NLAG // 2
    bins = (BAND0 + np.arange(GROUPS)[:, None, None] + 32 * np.arange(4)[None, None, :])
    phase = 2.0 * math.pi * (((lags[:, None, None, None] + M) * bins[None]) % M) / M
    both = np.concatenate([np.cos(phase), -np.sin(phase)], 2).reshape(NLAG, 2 * FB)
    rounded = both.astype(np.float32).astype(ml_dtypes.bfloat16).astype(np.float32)
    return (rounded / 64.0).astype(ml_dtypes.bfloat16)


def spread_table():
    table = np.zeros((CH, 2, 4, 2, CH), np.float32)
    for c in range(CH):
        for o in range(2):
            table[c, o, :, o, c] = 1.0
    return table.reshape(CH * 8, 2 * CH).astype(ml_dtypes.bfloat16)


def spectra_kernel(main_ref, tail_ref, quality_ref, first_ref, one_ref, two_ref, three_ref, halo_ref,
                   white_ref, turned_ref, held):
    step = pl.program_id(0)
    last = step == FRAMES // 2 - 1

    def transform(raw, after):
        both = lax.dot_general(main_ref[...], raw, NT, preferred_element_type=F32)
        ends = jnp.concatenate([after, after], 1)
        return (both[:ROWS] + both[ROWS:]) + lax.dot_general(
            tail_ref[...], ends, NT, preferred_element_type=F32)

    @pl.when(step == 0)
    def _():
        held[...] = transform(first_ref[...], one_ref[:, :128]).reshape(GROUPS + 2, 8, CH)

    two = jnp.where(last, halo_ref[:, :HALF], two_ref[...])
    three = jnp.where(last, halo_ref[:, HALF:], three_ref[...])
    raw = jnp.concatenate([one_ref[...], two], 0)
    after = jnp.concatenate([two[:, :128], three], 0)
    pair = transform(raw, after)
    zero = held[...]
    first = pair[:, :CH].reshape(GROUPS + 2, 8, CH)
    second = pair[:, CH:].reshape(GROUPS + 2, 8, CH)
    held[...] = second
    group = lax.broadcasted_iota(jnp.int32, (GROUPS, 8, CH), 0)
    odd = (group % 2) == 1
    row = lax.broadcasted_iota(jnp.int32, (GROUPS, 8, CH), 1)
    keep = quality_ref[...].reshape(1, 1, CH)

    def whiten(front, back):
        side = 0.25 * (front[:GROUPS] + front[2:])
        spec = 0.5 * front[1 : GROUPS + 1] - side
        other = 0.5 * back[1 : GROUPS + 1] + 0.25 * (back[:GROUPS] + back[2:])
        spec = spec + jnp.where(odd, -other, other)
        square = spec * spec
        level = jnp.sum(jnp.sum(square, 0), 0, keepdims=True).reshape(1, 1, CH) * (1.0 / FB)
        power = square + pltpu.roll(square, 4, 1)
        white = spec * lax.rsqrt(power + (0.1 * level + 1e-06)) * keep
        turned = pltpu.roll(white, 4, 1)
        return white, jnp.where(row < 4, turned, -turned)

    w0, t0 = whiten(zero, first)
    w1, t1 = whiten(first, second)
    white_ref[...] = jnp.concatenate([w0, w1], 1).astype(BF)
    turned_ref[...] = jnp.concatenate([t0, t1], 1).astype(BF)


def spectra(record, halo, quality):
    main, tail = half_tables()
    keep = quality.astype(F32).reshape(1, CH)
    whole = lambda *shape: pl.BlockSpec(shape, lambda i: (0,) * len(shape))
    out = jax.ShapeDtypeStruct((GROUPS, FRAMES * 8, CH), BF)
    return pl.pallas_call(
        spectra_kernel,
        grid=(FRAMES // 2,),
        out_shape=(out, out),
        in_specs=[
            whole(2 * ROWS, HALF),
            whole(ROWS, 256),
            whole(1, CH),
            pl.BlockSpec((CH, HALF), lambda i: (0, 0)),
            pl.BlockSpec((CH, HALF), lambda i: (0, 2 * i + 1)),
            pl.BlockSpec((CH, HALF), lambda i: (0, jnp.minimum(2 * i + 2, FRAMES - 1))),
            pl.BlockSpec((CH, 128), lambda i: (0, jnp.minimum((2 * i + 3) * 8, FRAMES * 8 - 1))),
            whole(CH, HALO),
        ],
        out_specs=[pl.BlockSpec((GROUPS, 16, CH), lambda i: (0, i, 0))] * 2,
        scratch_shapes=[pltpu.VMEM((GROUPS + 2, 8, CH), F32)],
        compiler_params=pltpu.CompilerParams(vmem_limit_bytes=40 * 2**20),
        name="spectra",
    )(jnp.asarray(main), jnp.asarray(tail), keep, record, record, record, record, halo)


CHUNKS = 16
SIZE = GROUPS // CHUNKS


def exchange_kernel(own_ref, got_ref, send_sem, recv_sem):
    me = lax.axis_index("blk")
    count = lax.axis_size("blk")
    ahead = lax.rem(me + 2, count)
    behind = lax.rem(me + count - 2, count)
    parity = lax.rem(me, 2)
    beside = me + 1 - 2 * parity
    barrier = pltpu.get_barrier_semaphore()
    for other in (ahead, behind, beside):
        pl.semaphore_signal(barrier, inc=1, device_id={"blk": other}, device_id_type=pl.DeviceIdType.MESH)
    pl.semaphore_wait(barrier, 3)

    def copy(source, which, target, slot, device):
        rows = pl.ds(which * SIZE, SIZE)
        src = own_ref.at[rows] if source == 0 else got_ref.at[source - 1, rows]
        return pltpu.make_async_remote_copy(
            src_ref=src,
            dst_ref=got_ref.at[target - 1, rows],
            send_sem=send_sem.at[slot, which],
            recv_sem=recv_sem.at[target - 1, which],
            device_id={"blk": device},
            device_id_type=pl.DeviceIdType.MESH,
        )

    def arrived(source, which):
        copy(0, which, source, 0, beside).wait_recv()

    half = CHUNKS // 2
    order = list(range(half, CHUNKS)) + list(range(half))

    @pl.when(parity == 0)
    def _():
        sent = []

        def send(*what):
            sent.append(copy(*what))
            sent[-1].start()

        for i in range(CHUNKS):
            send(0, order[i], 1, 0, beside)
            if i < half:
                send(0, i, 2, 1, ahead)
        for i in range(CHUNKS):
            arrived(1, i)
            send(1, i, 3, 2, ahead)
            if i < half:
                arrived(2, i)
                send(2, i, 3, 3, beside)
        for i in range(half, CHUNKS):
            arrived(2, i)
        for i in range(CHUNKS):
            arrived(3, i)
        for item in sent:
            item.wait_send()

    @pl.when(parity == 1)
    def _():
        sent = []

        def send(*what):
            sent.append(copy(*what))
            sent[-1].start()

        for i in range(CHUNKS):
            send(0, i, 2, 0, ahead)
        for i in range(CHUNKS):
            arrived(2, i)
            send(2, i, 1, 1, beside)
            if i < half:
                arrived(1, order[i])
                send(1, order[i], 3, 2, ahead)
        for i in range(half, CHUNKS):
            arrived(3, i)
            send(3, i, 2, 3, beside)
        for i in range(half):
            arrived(1, i)
        for i in range(half):
            arrived(3, i)
        for item in sent:
            item.wait_send()


def exchange(white):
    return pl.pallas_call(
        exchange_kernel,
        out_shape=jax.ShapeDtypeStruct((3,) + white.shape, white.dtype),
        in_specs=[pl.BlockSpec(memory_space=pl.ANY)],
        out_specs=pl.BlockSpec(memory_space=pl.ANY),
        scratch_shapes=[pltpu.SemaphoreType.DMA((4, CHUNKS)), pltpu.SemaphoreType.DMA((3, CHUNKS))],
        compiler_params=pltpu.CompilerParams(collective_id=0, has_side_effects=True),
        name="exchange",
    )(white)


CBLK = 32


def correlate_kernel(spread_ref, lag_ref, white_ref, turned_ref, got_ref, out_ref, cross):
    rows = lax.broadcasted_iota(jnp.int32, (CBLK * 8, 256), 0)
    cols = lax.broadcasted_iota(jnp.int32, (CBLK * 8, 256), 1)
    diagonal = (rows % 4) == (cols % 4)

    def stage(group):
        own = jnp.concatenate([white_ref[group], turned_ref[group]], 1)
        left = lax.dot_general(spread_ref[...], own, NT, preferred_element_type=F32)
        left = jnp.where(diagonal, left, 0.0).astype(BF)
        right = jnp.concatenate([white_ref[group]] + [got_ref[d, group] for d in range(3)], 1)
        return jnp.dot(left, right, preferred_element_type=F32).reshape(CBLK, 8, 4 * CH)

    @pl.loop(0, GROUPS // 2)
    def _(pair):
        both = jnp.concatenate([stage(2 * pair), stage(2 * pair + 1)], 1)
        cross[:, pl.ds(pl.multiple_of(pair * 16, 16), 16), :] = both.astype(BF)

    @pl.loop(0, CBLK)
    def _(c):
        result = jnp.dot(lag_ref[...], cross[c], preferred_element_type=F32)
        for d in range(4):
            flat = out_ref.at[d].reshape(NLAG * CBLK, CH)
            flat[pl.ds(c, NLAG, stride=CBLK), :] = result[:, d * CH : (d + 1) * CH]


def correlate(white, turned, got):
    whole = lambda *shape: pl.BlockSpec(shape, lambda i: (0,) * len(shape))
    spectrum = whole(GROUPS, 256, CH)
    return pl.pallas_call(
        correlate_kernel,
        grid=(CH // CBLK,),
        out_shape=jax.ShapeDtypeStruct((4, NLAG, CH, CH), F32),
        in_specs=[pl.BlockSpec((CBLK * 8, 256), lambda i: (i, 0)), whole(NLAG, 256)] + [spectrum] * 2 + [whole(3, GROUPS, 256, CH)],
        out_specs=pl.BlockSpec((4, NLAG, CBLK, CH), lambda i: (0, 0, i, 0)),
        scratch_shapes=[pltpu.VMEM((CBLK, 256, 4 * CH), BF)],
        compiler_params=pltpu.CompilerParams(vmem_limit_bytes=60 * 2**20),
        name="correlate",
    )(jnp.asarray(spread_table()), jnp.asarray(lag_table()), white, turned, got)


def shards(record, quality):
    count = lax.axis_size("pre")
    halo = lax.ppermute(record[:, :HALO], "pre", [(i, i - 1) for i in range(1, count)])
    white, turned = spectra(record, halo, quality)
    return correlate(white, turned, exchange(white))[None]


def solution(mesh):
    placed = (P("blk", "pre"), P("blk"))
    return jax.shard_map(
        shards,
        mesh=mesh,
        in_specs=placed,
        out_specs=P("pre", None, None, "blk", None),
        check_vma=False,
    )
```

```python
import math

import jax
import jax.numpy as jnp
import ml_dtypes
import numpy as np
from jax import lax
from jax.experimental import pallas as pl
from jax.experimental.pallas import tpu as pltpu
from jax.sharding import PartitionSpec as P

M = 512
R = 4
KT = 16
FB = 128
NLAG = 64
BAND0 = 16
CH = 128
HALF = 1024
FRAMES = 32
GROUPS = 32
ROWS = (GROUPS + 2) * 8
HALO = HALF + 128
NT = (((1,), (1,)), ((), ()))
BF = jnp.bfloat16
F32 = jnp.float32


def filter_taps():
    index = np.arange(KT, dtype=np.float32)
    centre = np.float32((KT - 1) / 2.0)
    shaped = np.sinc((index - centre) / np.float32(R)) * (
        0.54 - 0.46 * np.cos(2.0 * math.pi * index / (KT - 1))
    )
    return (shaped / np.sum(shaped)).astype(np.float32).astype(ml_dtypes.bfloat16)


def split(table):
    high = table.astype(np.float32).astype(ml_dtypes.bfloat16)
    low = (table - high.astype(np.float64)).astype(np.float32).astype(ml_dtypes.bfloat16)
    return high, low


def half_tables():
    taps = filter_taps().astype(np.float64)
    toeplitz = np.zeros((M // 2, HALF + 128))
    for m in range(M // 2):
        toeplitz[m, R * m : R * m + KT] = taps
    group = np.arange(-1, GROUPS + 1)
    bins = BAND0 + group[:, None] + 32 * np.arange(4)[None, :]
    phase = 2.0 * math.pi * ((bins[:, :, None] * np.arange(M // 2)) % M) / M
    both = np.stack([np.cos(phase), -np.sin(phase)], 1).reshape(ROWS, M // 2)
    table = both @ toeplitz
    high, low = split(table)
    main = np.concatenate([high[:, :HALF], low[:, :HALF]], 0)
    tail = np.concatenate([high[:, HALF:], low[:, HALF:]], 1)
    return main, tail


def lag_table():
    lags = np.arange(NLAG) - NLAG // 2
    bins = (BAND0 + np.arange(GROUPS)[:, None, None] + 32 * np.arange(4)[None, None, :])
    phase = 2.0 * math.pi * (((lags[:, None, None, None] + M) * bins[None]) % M) / M
    both = np.concatenate([np.cos(phase), -np.sin(phase)], 2).reshape(NLAG, 2 * FB)
    rounded = both.astype(np.float32).astype(ml_dtypes.bfloat16).astype(np.float32)
    return (rounded / 64.0).astype(ml_dtypes.bfloat16)


def spread_table():
    table = np.zeros((CH, 2, 4, 2, CH), np.float32)
    for c in range(CH):
        for o in range(2):
            table[c, o, :, o, c] = 1.0
    return table.reshape(CH * 8, 2 * CH).astype(ml_dtypes.bfloat16)


def spectra_kernel(main_ref, tail_ref, quality_ref, first_ref, one_ref, two_ref, three_ref, halo_ref,
                   white_ref, turned_ref, held):
    step = pl.program_id(0)
    last = step == FRAMES // 2 - 1

    def transform(raw, after):
        both = lax.dot_general(main_ref[...], raw, NT, preferred_element_type=F32)
        ends = jnp.concatenate([after, after], 1)
        return (both[:ROWS] + both[ROWS:]) + lax.dot_general(
            tail_ref[...], ends, NT, preferred_element_type=F32)

    @pl.when(step == 0)
    def _():
        held[...] = transform(first_ref[...], one_ref[:, :128]).reshape(GROUPS + 2, 8, CH)

    two = jnp.where(last, halo_ref[:, :HALF], two_ref[...])
    three = jnp.where(last, halo_ref[:, HALF:], three_ref[...])
    raw = jnp.concatenate([one_ref[...], two], 0)
    after = jnp.concatenate([two[:, :128], three], 0)
    pair = transform(raw, after)
    zero = held[...]
    first = pair[:, :CH].reshape(GROUPS + 2, 8, CH)
    second = pair[:, CH:].reshape(GROUPS + 2, 8, CH)
    held[...] = second
    group = lax.broadcasted_iota(jnp.int32, (GROUPS, 8, CH), 0)
    odd = (group % 2) == 1
    row = lax.broadcasted_iota(jnp.int32, (GROUPS, 8, CH), 1)
    keep = quality_ref[...].reshape(1, 1, CH)

    def whiten(front, back):
        side = 0.25 * (front[:GROUPS] + front[2:])
        spec = 0.5 * front[1 : GROUPS + 1] - side
        other = 0.5 * back[1 : GROUPS + 1] + 0.25 * (back[:GROUPS] + back[2:])
        spec = spec + jnp.where(odd, -other, other)
        square = spec * spec
        level = jnp.sum(jnp.sum(square, 0), 0, keepdims=True).reshape(1, 1, CH) * (1.0 / FB)
        power = square + pltpu.roll(square, 4, 1)
        white = spec * lax.rsqrt(power + (0.1 * level + 1e-06)) * keep
        turned = pltpu.roll(white, 4, 1)
        return white, jnp.where(row < 4, turned, -turned)

    w0, t0 = whiten(zero, first)
    w1, t1 = whiten(first, second)
    white_ref[...] = jnp.concatenate([w0, w1], 1).astype(BF)
    turned_ref[...] = jnp.concatenate([t0, t1], 1).astype(BF)


def spectra(record, halo, quality):
    main, tail = half_tables()
    keep = quality.astype(F32).reshape(1, CH)
    whole = lambda *shape: pl.BlockSpec(shape, lambda i: (0,) * len(shape))
    out = jax.ShapeDtypeStruct((GROUPS, FRAMES * 8, CH), BF)
    return pl.pallas_call(
        spectra_kernel,
        grid=(FRAMES // 2,),
        out_shape=(out, out),
        in_specs=[
            whole(2 * ROWS, HALF),
            whole(ROWS, 256),
            whole(1, CH),
            pl.BlockSpec((CH, HALF), lambda i: (0, 0)),
            pl.BlockSpec((CH, HALF), lambda i: (0, 2 * i + 1)),
            pl.BlockSpec((CH, HALF), lambda i: (0, jnp.minimum(2 * i + 2, FRAMES - 1))),
            pl.BlockSpec((CH, 128), lambda i: (0, jnp.minimum((2 * i + 3) * 8, FRAMES * 8 - 1))),
            whole(CH, HALO),
        ],
        out_specs=[pl.BlockSpec((GROUPS, 16, CH), lambda i: (0, i, 0))] * 2,
        scratch_shapes=[pltpu.VMEM((GROUPS + 2, 8, CH), F32)],
        compiler_params=pltpu.CompilerParams(vmem_limit_bytes=60 * 2**20),
        name="spectra",
    )(jnp.asarray(main), jnp.asarray(tail), keep, record, record, record, record, halo)


CHUNKS = GROUPS // 2
PART = 32


def exchange_kernel(spread_ref, lag_ref, white_ref, turned_ref, near_ref, far_ref,
                    got, left, cross, fars, nears, send_sem, recv_sem, far_sem, near_sem):
    me = lax.axis_index("blk")
    count = lax.axis_size("blk")
    ahead = lax.rem(me + 2, count)
    behind = lax.rem(me + count - 2, count)
    parity = lax.rem(me, 2)
    beside = me + 1 - 2 * parity
    barrier = pltpu.get_barrier_semaphore()
    for other in (ahead, behind, beside):
        pl.semaphore_signal(barrier, inc=1, device_id={"blk": other}, device_id_type=pl.DeviceIdType.MESH)
    pl.semaphore_wait(barrier, 3)

    def copy(source, which, target, slot, device):
        rows = pl.ds(which * 2, 2)
        src = white_ref.at[rows] if source == 0 else got.at[source - 1, rows]
        return pltpu.make_async_remote_copy(
            src_ref=src,
            dst_ref=got.at[target - 1, rows],
            send_sem=send_sem.at[slot, which],
            recv_sem=recv_sem.at[target - 1, which],
            device_id={"blk": device},
            device_id_type=pl.DeviceIdType.MESH,
        )

    def arrived(source, which):
        copy(0, which, source, 0, beside).wait_recv()

    @pl.when(parity == 0)
    def _():
        for i in range(CHUNKS):
            copy(0, i, 1, 0, beside).start()
            if i % 2 == 0:
                copy(0, i, 2, 1, ahead).start()

    @pl.when(parity == 1)
    def _():
        for i in range(CHUNKS):
            copy(0, i, 2, 0, ahead).start()

    rows = lax.broadcasted_iota(jnp.int32, (PART * 8, 256), 0)
    cols = lax.broadcasted_iota(jnp.int32, (PART * 8, 256), 1)
    diagonal = (rows % 4) == (cols % 4)

    @pl.loop(0, CHUNKS)
    def _(p):
        even = lax.rem(p, 2) == 0

        @pl.when(parity == 0)
        def _():
            arrived(1, p)
            copy(1, p, 3, 2, ahead).start()

            @pl.when(even)
            def _():
                arrived(2, p)
                copy(2, p, 3, 3, beside).start()

        @pl.when(parity == 1)
        def _():
            arrived(2, p)
            copy(2, p, 1, 1, beside).start()
            arrived(1, p)

            @pl.when(jnp.logical_not(even))
            def _():
                copy(1, p, 3, 2, ahead).start()

        for part in range(CH // PART):
            lines = pl.ds(part * PART * 8, PART * 8)
            pieces = []
            for j in range(2):
                group = 2 * p + j
                own = jnp.concatenate([white_ref[group], turned_ref[group]], 1)
                table = lax.dot_general(spread_ref[lines, :], own, NT, preferred_element_type=F32)
                table = jnp.where(diagonal, table, 0.0).astype(BF)
                left[group, lines, :] = table
                right = jnp.concatenate([white_ref[group], got[0, group]], 1)
                pieces.append(jnp.dot(table, right, preferred_element_type=F32).reshape(PART, 8, 2 * CH))
            both = jnp.concatenate(pieces, 1).astype(BF)
            cross[pl.ds(part * PART, PART), pl.ds(pl.multiple_of(p * 16, 16), 16), :] = both

    def store_far(p):
        at = pl.ds(pl.multiple_of(p * 16, 16), 16)
        return pltpu.make_async_copy(fars.at[lax.rem(p, 2)], far_ref.at[:, at, :], far_sem.at[lax.rem(p, 2)])

    def store_near(p):
        at = pl.ds(pl.multiple_of(p * 8, 8), 8)
        return pltpu.make_async_copy(nears.at[lax.rem(p, 2)], near_ref.at[:, :, at, :], near_sem.at[lax.rem(p, 2)])

    @pl.loop(0, CHUNKS)
    def _(p):
        even = lax.rem(p, 2) == 0
        buffer = lax.rem(p, 2)

        @pl.when(parity == 0)
        def _():
            arrived(3, p)

            @pl.when(jnp.logical_not(even))
            def _():
                arrived(2, p)

        @pl.when(parity == 1)
        def _():
            arrived(3, p)

            @pl.when(jnp.logical_not(even))
            def _():
                copy(3, p, 2, 3, beside).start()

        @pl.when(p >= 2)
        def _():
            store_far(p - 2).wait()
            store_near(p - 2).wait()

        for part in range(CH // PART):
            lines = pl.ds(part * PART * 8, PART * 8)
            pieces = []
            for j in range(2):
                group = 2 * p + j
                right = jnp.concatenate([got[1, group], got[2, group]], 1)
                pieces.append(
                    jnp.dot(left[group, lines, :], right, preferred_element_type=F32).reshape(PART, 8, 2 * CH))
            fars[buffer, pl.ds(part * PART, PART)] = jnp.concatenate(pieces, 1).astype(BF)
        store_far(p).start()

        for j in range(8):
            result = jnp.dot(lag_ref[...], cross[p * 8 + j], preferred_element_type=F32)
            for d in range(2):
                flat = nears.at[buffer, d].reshape(NLAG * 8, CH)
                flat[pl.ds(j, NLAG, stride=8), :] = result[:, d * CH : (d + 1) * CH]
        store_near(p).start()

    for p in (CHUNKS - 2, CHUNKS - 1):
        store_far(p).wait()
        store_near(p).wait()

    @pl.loop(0, CHUNKS)
    def _(p):
        even = lax.rem(p, 2) == 0

        @pl.when(parity == 0)
        def _():
            copy(0, p, 1, 0, beside).wait_send()
            copy(1, p, 3, 2, ahead).wait_send()

            @pl.when(even)
            def _():
                copy(0, p, 2, 1, ahead).wait_send()
                copy(2, p, 3, 3, beside).wait_send()

        @pl.when(parity == 1)
        def _():
            copy(0, p, 2, 0, ahead).wait_send()
            copy(2, p, 1, 1, beside).wait_send()

            @pl.when(jnp.logical_not(even))
            def _():
                copy(1, p, 3, 2, ahead).wait_send()
                copy(3, p, 2, 3, beside).wait_send()


def exchange(white, turned):
    inside = pl.BlockSpec(memory_space=pltpu.VMEM)
    return pl.pallas_call(
        exchange_kernel,
        out_shape=(
            jax.ShapeDtypeStruct((2, NLAG, CH, CH), F32),
            jax.ShapeDtypeStruct((CH, 2 * FB, 2 * CH), BF),
        ),
        in_specs=[inside] * 4,
        out_specs=(pl.BlockSpec(memory_space=pl.ANY),) * 2,
        scratch_shapes=[
            pltpu.VMEM((3, GROUPS, 256, CH), BF),
            pltpu.VMEM((GROUPS, CH * 8, 256), BF),
            pltpu.VMEM((CH, 2 * FB, 2 * CH), BF),
            pltpu.VMEM((2, CH, 16, 2 * CH), BF),
            pltpu.VMEM((2, 2, NLAG, 8, CH), F32),
            pltpu.SemaphoreType.DMA((4, CHUNKS)),
            pltpu.SemaphoreType.DMA((3, CHUNKS)),
            pltpu.SemaphoreType.DMA((2,)),
            pltpu.SemaphoreType.DMA((2,)),
        ],
        compiler_params=pltpu.CompilerParams(
            collective_id=0, has_side_effects=True, vmem_limit_bytes=60 * 2**20),
        name="exchange",
    )(jnp.asarray(spread_table()), jnp.asarray(lag_table()), white, turned)


LAST = 16


def last_kernel(lag_ref, near_ref, far_ref, out_ref):
    out_ref[0:2] = near_ref[...]

    @pl.loop(0, LAST // 8)
    def _(step):
        for j in range(8):
            c = step * 8 + j
            result = jnp.dot(lag_ref[...], far_ref[c], preferred_element_type=F32)
            for d in range(2):
                flat = out_ref.at[2 + d].reshape(NLAG * LAST, CH)
                flat[pl.ds(c, NLAG, stride=LAST), :] = result[:, d * CH : (d + 1) * CH]


def last(near, far):
    return pl.pallas_call(
        last_kernel,
        grid=(CH // LAST,),
        out_shape=jax.ShapeDtypeStruct((4, NLAG, CH, CH), F32),
        in_specs=[
            pl.BlockSpec((NLAG, 2 * FB), lambda i: (0, 0)),
            pl.BlockSpec((2, NLAG, LAST, CH), lambda i: (0, 0, i, 0)),
            pl.BlockSpec((LAST, 2 * FB, 2 * CH), lambda i: (i, 0, 0)),
        ],
        out_specs=pl.BlockSpec((4, NLAG, LAST, CH), lambda i: (0, 0, i, 0)),
        compiler_params=pltpu.CompilerParams(vmem_limit_bytes=60 * 2**20),
        name="last",
    )(jnp.asarray(lag_table()), near, far)


def shards(record, quality):
    count = lax.axis_size("pre")
    halo = lax.ppermute(record[:, :HALO], "pre", [(i, i - 1) for i in range(1, count)])
    white, turned = spectra(record, halo, quality)
    return last(*exchange(white, turned))[None]


def solution(mesh):
    placed = (P("blk", "pre"), P("blk"))
    return jax.shard_map(
        shards,
        mesh=mesh,
        in_specs=placed,
        out_specs=P("pre", None, None, "blk", None),
        check_vma=False,
    )
```

```python
import math

import jax
import jax.numpy as jnp
import ml_dtypes
import numpy as np
from jax import lax
from jax.experimental import pallas as pl
from jax.experimental.pallas import tpu as pltpu
from jax.sharding import PartitionSpec as P

M = 512
R = 4
KT = 16
FB = 128
NLAG = 64
BAND0 = 16
CH = 128
HALF = 1024
FRAMES = 32
GROUPS = 32
ROWS = (GROUPS + 2) * 8
HALO = HALF + 128
NT = (((1,), (1,)), ((), ()))
BF = jnp.bfloat16
F32 = jnp.float32


def filter_taps():
    index = np.arange(KT, dtype=np.float32)
    centre = np.float32((KT - 1) / 2.0)
    shaped = np.sinc((index - centre) / np.float32(R)) * (
        0.54 - 0.46 * np.cos(2.0 * math.pi * index / (KT - 1))
    )
    return (shaped / np.sum(shaped)).astype(np.float32).astype(ml_dtypes.bfloat16)


def split(table):
    high = table.astype(np.float32).astype(ml_dtypes.bfloat16)
    low = (table - high.astype(np.float64)).astype(np.float32).astype(ml_dtypes.bfloat16)
    return high, low


def half_tables():
    taps = filter_taps().astype(np.float64)
    toeplitz = np.zeros((M // 2, HALF + 128))
    for m in range(M // 2):
        toeplitz[m, R * m : R * m + KT] = taps
    group = np.arange(-1, GROUPS + 1)
    bins = BAND0 + group[:, None] + 32 * np.arange(4)[None, :]
    phase = 2.0 * math.pi * ((bins[:, :, None] * np.arange(M // 2)) % M) / M
    both = np.stack([np.cos(phase), -np.sin(phase)], 1).reshape(ROWS, M // 2)
    table = both @ toeplitz
    high, low = split(table)
    main = np.concatenate([high[:, :HALF], low[:, :HALF]], 0)
    tail = np.concatenate([high[:, HALF:], low[:, HALF:]], 1)
    return main, tail


def lag_table():
    lags = np.arange(NLAG) - NLAG // 2
    bins = (BAND0 + np.arange(GROUPS)[:, None, None] + 32 * np.arange(4)[None, None, :])
    phase = 2.0 * math.pi * (((lags[:, None, None, None] + M) * bins[None]) % M) / M
    both = np.concatenate([np.cos(phase), -np.sin(phase)], 2).reshape(NLAG, 2 * FB)
    rounded = both.astype(np.float32).astype(ml_dtypes.bfloat16).astype(np.float32)
    return (rounded / 64.0).astype(ml_dtypes.bfloat16)


def spread_table():
    table = np.zeros((CH, 2, 4, 2, CH), np.float32)
    for c in range(CH):
        for o in range(2):
            table[c, o, :, o, c] = 1.0
    return table.reshape(CH * 8, 2 * CH).astype(ml_dtypes.bfloat16)


CHUNKS = 16
PART = 32
LENGTH = FRAMES * HALF


def exchange_kernel(record_ref, quality_ref, main_hbm, tail_hbm, spread_hbm, lag_hbm, near_ref, far_ref,
                    rec, main, tail, spread, lag, held, white, turned, got, left, cross, fars, nears,
                    send_sem, recv_sem, far_sem, near_sem, rec_sem, table_sem, halo_sem):
    tables = [
        pltpu.make_async_copy(source, target, table_sem.at[i])
        for i, (source, target) in enumerate(
            [(main_hbm, main), (tail_hbm, tail), (spread_hbm, spread), (lag_hbm, lag)])
    ]

    def piece(i):
        at = pl.ds(pl.multiple_of(i * 2 * HALF, 2 * HALF), 2 * HALF)
        return pltpu.make_async_copy(record_ref.at[:, at], rec.at[:, at], rec_sem.at[i])

    piece(0).start()
    tables[0].start()
    tables[1].start()
    for i in range(1, FRAMES // 2):
        piece(i).start()
    tables[2].start()
    tables[3].start()

    me = lax.axis_index("blk")
    count = lax.axis_size("blk")
    ahead = lax.rem(me + 2, count)
    behind = lax.rem(me + count - 2, count)
    parity = lax.rem(me, 2)
    beside = me + 1 - 2 * parity
    segment = lax.axis_index("pre")
    segments = lax.axis_size("pre")
    sooner = lax.rem(segment + segments - 1, segments)
    later = lax.rem(segment + 1, segments)
    barrier = pltpu.get_barrier_semaphore()
    for other in (ahead, behind, beside):
        pl.semaphore_signal(barrier, inc=1, device_id={"blk": other}, device_id_type=pl.DeviceIdType.MESH)
    for other in (sooner, later):
        pl.semaphore_signal(barrier, inc=1, device_id={"pre": other}, device_id_type=pl.DeviceIdType.MESH)
    pl.semaphore_wait(barrier, 5)

    halo = pltpu.make_async_remote_copy(
        src_ref=record_ref.at[:, pl.ds(0, HALO)],
        dst_ref=rec.at[:, pl.ds(LENGTH, HALO)],
        send_sem=halo_sem.at[0],
        recv_sem=halo_sem.at[1],
        device_id={"pre": sooner},
        device_id_type=pl.DeviceIdType.MESH,
    )

    @pl.when(segment > 0)
    def _():
        halo.start()

    @pl.when(segment == segments - 1)
    def _():
        rec[:, LENGTH:] = jnp.zeros((CH, HALO), BF)

    def view(ref, half, which):
        if half == 0:
            return ref.at[:, pl.ds(pl.multiple_of(which * 16, 16), 16), :]
        return ref.at[pl.ds(which * 4, 4), pl.ds(128, 128), :]

    def copy(half, which, source, target, slot, device):
        return pltpu.make_async_remote_copy(
            src_ref=view(white if source == 0 else got.at[source - 1], half, which),
            dst_ref=view(got.at[target - 1], half, which),
            send_sem=send_sem.at[slot, half * 8 + which],
            recv_sem=recv_sem.at[target - 1, half * 8 + which],
            device_id={"blk": device},
            device_id_type=pl.DeviceIdType.MESH,
        )

    def arrived(half, which, source):
        copy(half, which, 0, source, 0, beside).wait_recv()

    def on(condition):
        return lambda body: pl.when(condition)(body)

    def offer(half, which):
        @on(parity == 0)
        def _():
            copy(half, which, 0, 1, 0, beside).start()

            @on(lax.rem(which, 2) == 0)
            def _():
                copy(half, which, 0, 2, 1, ahead).start()

        @on(parity == 1)
        def _():
            copy(half, which, 0, 2, 0, ahead).start()

    def relay(half, which):
        @on(parity == 0)
        def _():
            arrived(half, which, 1)
            copy(half, which, 1, 3, 2, ahead).start()

            @on(lax.rem(which, 2) == 0)
            def _():
                arrived(half, which, 2)
                copy(half, which, 2, 3, 3, beside).start()

        @on(parity == 1)
        def _():
            arrived(half, which, 2)
            copy(half, which, 2, 1, 1, beside).start()
            arrived(half, which, 1)

            @on(lax.rem(which, 2) == 1)
            def _():
                copy(half, which, 1, 3, 2, ahead).start()

    def finish(half, which):
        arrived(half, which, 3)

        @on(lax.rem(which, 2) == 1)
        def _():
            @on(parity == 0)
            def _():
                arrived(half, which, 2)

            @on(parity == 1)
            def _():
                copy(half, which, 3, 2, 3, beside).start()

    def transform(raw, after):
        both = lax.dot_general(main[...], raw, NT, preferred_element_type=F32)
        ends = jnp.concatenate([after, after], 1)
        return (both[:ROWS] + both[ROWS:]) + lax.dot_general(
            tail[...], ends, NT, preferred_element_type=F32)

    piece(0).wait()
    tables[0].wait()
    tables[1].wait()
    held[...] = transform(rec[:, :HALF], rec[:, HALF : HALF + 128]).reshape(GROUPS + 2, 8, CH)
    keep = quality_ref[...].astype(F32).reshape(1, 1, CH)

    def frames(step):
        start = pl.multiple_of(step * 2 * HALF + HALF, HALF)
        one = pl.ds(start, HALF)
        two = pl.ds(pl.multiple_of(start + HALF, HALF), HALF)
        raw = jnp.concatenate([rec[:, one], rec[:, two]], 0)
        after = jnp.concatenate([
            rec[:, pl.ds(pl.multiple_of(start + HALF, HALF), 128)],
            rec[:, pl.ds(pl.multiple_of(start + 2 * HALF, HALF), 128)]], 0)
        pair = transform(raw, after)
        zero = held[...]
        first = pair[:, :CH].reshape(GROUPS + 2, 8, CH)
        second = pair[:, CH:].reshape(GROUPS + 2, 8, CH)
        held[...] = second
        group = lax.broadcasted_iota(jnp.int32, (GROUPS, 8, CH), 0)
        odd = (group % 2) == 1
        row = lax.broadcasted_iota(jnp.int32, (GROUPS, 8, CH), 1)

        def whiten(front, back):
            side = 0.25 * (front[:GROUPS] + front[2:])
            spec = 0.5 * front[1 : GROUPS + 1] - side
            other = 0.5 * back[1 : GROUPS + 1] + 0.25 * (back[:GROUPS] + back[2:])
            spec = spec + jnp.where(odd, -other, other)
            square = spec * spec
            level = jnp.sum(jnp.sum(square, 0), 0, keepdims=True).reshape(1, 1, CH) * (1.0 / FB)
            power = square + pltpu.roll(square, 4, 1)
            plain = spec * lax.rsqrt(power + (0.1 * level + 1e-06)) * keep
            swapped = pltpu.roll(plain, 4, 1)
            return plain, jnp.where(row < 4, swapped, -swapped)

        w0, t0 = whiten(zero, first)
        w1, t1 = whiten(first, second)
        at = pl.ds(pl.multiple_of(step * 16, 16), 16)
        white[:, at, :] = jnp.concatenate([w0, w1], 1).astype(BF)
        turned[:, at, :] = jnp.concatenate([t0, t1], 1).astype(BF)

    @pl.loop(0, 8)
    def _(step):
        piece(step + 1).wait()
        frames(step)
        offer(0, step)

    @pl.loop(8, FRAMES // 2)
    def _(step):
        @on(step < FRAMES // 2 - 1)
        def _():
            piece(step + 1).wait()

        @on(jnp.logical_and(step == FRAMES // 2 - 1, segment < segments - 1))
        def _():
            halo.wait_recv()

        frames(step)

        @on(lax.rem(step, 3) == 0)
        def _():
            relay(0, lax.div(step, 3) - 3)

    @pl.loop(0, 8)
    def _(which):
        offer(1, which)

    tables[2].wait()
    tables[3].wait()
    rows = lax.broadcasted_iota(jnp.int32, (PART * 8, 256), 0)
    cols = lax.broadcasted_iota(jnp.int32, (PART * 8, 256), 1)
    diagonal = (rows % 4) == (cols % 4)

    @pl.loop(3, 8)
    def _(which):
        relay(0, which)

        @on(which < 7)
        def _():
            @pl.loop(0, 8)
            def _(j):
                group = (which - 3) * 8 + j
                own = jnp.concatenate([white[group], turned[group]], 1)
                for part in range(CH // PART):
                    lines = pl.ds(part * PART * 8, PART * 8)
                    table = lax.dot_general(spread[lines, :], own, NT, preferred_element_type=F32)
                    left[group, lines, :] = jnp.where(diagonal, table, 0.0).astype(BF)

    def products(pair, one, two, store):
        for part in range(CH // PART):
            lines = pl.ds(part * PART * 8, PART * 8)
            pieces = []
            for j in range(2):
                group = 2 * pair + j
                right = jnp.concatenate([one[group], two[group]], 1)
                pieces.append(
                    jnp.dot(left[group, lines, :], right, preferred_element_type=F32).reshape(PART, 8, 2 * CH))
            store(part, jnp.concatenate(pieces, 1).astype(BF))

    @pl.loop(0, 8)
    def _(which):
        relay(1, which)

        @pl.loop(0, 2)
        def _(j):
            pair = which * 2 + j

            def store(part, value):
                cross[pl.ds(part * PART, PART), pl.ds(pl.multiple_of(pair * 16, 16), 16), :] = value

            products(pair, white, got.at[0], store)

    def store_far(which):
        at = pl.ds(pl.multiple_of(which * 32, 32), 32)
        buffer = lax.rem(which, 2)
        return pltpu.make_async_copy(fars.at[buffer], far_ref.at[:, at, :], far_sem.at[buffer])

    def store_near(which):
        at = pl.ds(pl.multiple_of(which * 8, 8), 8)
        buffer = lax.rem(which, 2)
        return pltpu.make_async_copy(nears.at[buffer], near_ref.at[:, :, at, :], near_sem.at[buffer])

    @pl.loop(0, 8)
    def _(which):
        finish(0, which)
        for buffer in range(2):
            step = which * 2 + buffer

            @on(which > 0)
            def _():
                store_near(step - 2).wait()

            for j in range(8):
                result = jnp.dot(lag[...], cross[step * 8 + j], preferred_element_type=F32)
                for d in range(2):
                    flat = nears.at[buffer, d].reshape(NLAG * 8, CH)
                    flat[pl.ds(j, NLAG, stride=8), :] = result[:, d * CH : (d + 1) * CH]
            store_near(step).start()

    @pl.loop(0, 8)
    def _(which):
        finish(1, which)

        @on(which > 1)
        def _():
            store_far(which - 2).wait()

        @pl.loop(0, 2)
        def _(j):
            def store(part, value):
                fars[lax.rem(which, 2), pl.ds(part * PART, PART),
                     pl.ds(pl.multiple_of(j * 16, 16), 16), :] = value

            products(which * 2 + j, got.at[1], got.at[2], store)

        store_far(which).start()

    for step in (CHUNKS - 2, CHUNKS - 1):
        store_near(step).wait()
    for which in (6, 7):
        store_far(which).wait()

    @on(segment > 0)
    def _():
        halo.wait_send()

    for half in range(2):
        @pl.loop(0, 8)
        def _(which):
            copy(half, which, 0, 1, 0, beside).wait_send()

            @on(parity == 0)
            def _():
                copy(half, which, 1, 3, 2, ahead).wait_send()

                @on(lax.rem(which, 2) == 0)
                def _():
                    copy(half, which, 0, 2, 1, ahead).wait_send()
                    copy(half, which, 2, 3, 3, beside).wait_send()

            @on(parity == 1)
            def _():
                copy(half, which, 2, 1, 1, beside).wait_send()

                @on(lax.rem(which, 2) == 1)
                def _():
                    copy(half, which, 1, 3, 2, ahead).wait_send()
                    copy(half, which, 3, 2, 3, beside).wait_send()


def exchange(record, quality):
    tables = [jnp.asarray(t) for t in half_tables() + (spread_table(), lag_table())]
    anywhere = pl.BlockSpec(memory_space=pl.ANY)
    return pl.pallas_call(
        exchange_kernel,
        out_shape=(
            jax.ShapeDtypeStruct((2, NLAG, CH, CH), F32),
            jax.ShapeDtypeStruct((CH, 2 * FB, 2 * CH), BF),
        ),
        in_specs=[anywhere, pl.BlockSpec(memory_space=pltpu.VMEM)] + [anywhere] * 4,
        out_specs=(anywhere,) * 2,
        scratch_shapes=[
            pltpu.VMEM((CH, LENGTH + HALO), BF),
            pltpu.VMEM((2 * ROWS, HALF), BF),
            pltpu.VMEM((ROWS, 256), BF),
            pltpu.VMEM((CH * 8, 256), BF),
            pltpu.VMEM((NLAG, 2 * FB), BF),
            pltpu.VMEM((GROUPS + 2, 8, CH), F32),
            pltpu.VMEM((GROUPS, 256, CH), BF),
            pltpu.VMEM((GROUPS, 256, CH), BF),
            pltpu.VMEM((3, GROUPS, 256, CH), BF),
            pltpu.VMEM((GROUPS, CH * 8, 256), BF),
            pltpu.VMEM((CH, 2 * FB, 2 * CH), BF),
            pltpu.VMEM((2, CH, 32, 2 * CH), BF),
            pltpu.VMEM((2, 2, NLAG, 8, CH), F32),
            pltpu.SemaphoreType.DMA((4, CHUNKS)),
            pltpu.SemaphoreType.DMA((3, CHUNKS)),
            pltpu.SemaphoreType.DMA((2,)),
            pltpu.SemaphoreType.DMA((2,)),
            pltpu.SemaphoreType.DMA((FRAMES // 2,)),
            pltpu.SemaphoreType.DMA((4,)),
            pltpu.SemaphoreType.DMA((2,)),
        ],
        compiler_params=pltpu.CompilerParams(
            collective_id=0, has_side_effects=True, vmem_limit_bytes=61 * 2**20),
        name="exchange",
    )(record, quality.reshape(1, CH), *tables)


LAST = 16


def last_kernel(lag_ref, near_ref, far_ref, out_ref):
    out_ref[0:2] = near_ref[...]

    @pl.loop(0, LAST // 8)
    def _(step):
        for j in range(8):
            c = step * 8 + j
            result = jnp.dot(lag_ref[...], far_ref[c], preferred_element_type=F32)
            for d in range(2):
                flat = out_ref.at[2 + d].reshape(NLAG * LAST, CH)
                flat[pl.ds(c, NLAG, stride=LAST), :] = result[:, d * CH : (d + 1) * CH]


def last(near, far):
    return pl.pallas_call(
        last_kernel,
        grid=(CH // LAST,),
        out_shape=jax.ShapeDtypeStruct((4, NLAG, CH, CH), F32),
        in_specs=[
            pl.BlockSpec((NLAG, 2 * FB), lambda i: (0, 0)),
            pl.BlockSpec((2, NLAG, LAST, CH), lambda i: (0, 0, i, 0)),
            pl.BlockSpec((LAST, 2 * FB, 2 * CH), lambda i: (i, 0, 0)),
        ],
        out_specs=pl.BlockSpec((4, NLAG, LAST, CH), lambda i: (0, 0, i, 0)),
        compiler_params=pltpu.CompilerParams(vmem_limit_bytes=60 * 2**20),
        name="last",
    )(jnp.asarray(lag_table()), near, far)


def shards(record, quality):
    return last(*exchange(record, quality))[None]


def solution(mesh):
    placed = (P("blk", "pre"), P("blk"))
    return jax.shard_map(
        shards,
        mesh=mesh,
        in_specs=placed,
        out_specs=P("pre", None, None, "blk", None),
        check_vma=False,
    )
```

```python
import math

import jax
import jax.numpy as jnp
import ml_dtypes
import numpy as np
from jax import lax
from jax.experimental import pallas as pl
from jax.experimental.pallas import tpu as pltpu
from jax.sharding import PartitionSpec as P

M = 512
R = 4
KT = 16
FB = 128
NLAG = 64
BAND0 = 16
CH = 128
HALF = 1024
FRAMES = 32
GROUPS = 32
ROWS = (GROUPS + 2) * 8
HALO = HALF + 128
NT = (((1,), (1,)), ((), ()))
BF = jnp.bfloat16
F32 = jnp.float32


def filter_taps():
    index = np.arange(KT, dtype=np.float32)
    centre = np.float32((KT - 1) / 2.0)
    shaped = np.sinc((index - centre) / np.float32(R)) * (
        0.54 - 0.46 * np.cos(2.0 * math.pi * index / (KT - 1))
    )
    return (shaped / np.sum(shaped)).astype(np.float32).astype(ml_dtypes.bfloat16)


def split(table):
    high = table.astype(np.float32).astype(ml_dtypes.bfloat16)
    low = (table - high.astype(np.float64)).astype(np.float32).astype(ml_dtypes.bfloat16)
    return high, low


def half_tables():
    taps = filter_taps().astype(np.float64)
    toeplitz = np.zeros((M // 2, HALF + 128))
    for m in range(M // 2):
        toeplitz[m, R * m : R * m + KT] = taps
    group = np.arange(-1, GROUPS + 1)
    bins = BAND0 + group[:, None] + 32 * np.arange(4)[None, :]
    phase = 2.0 * math.pi * ((bins[:, :, None] * np.arange(M // 2)) % M) / M
    both = np.stack([np.cos(phase), -np.sin(phase)], 1).reshape(ROWS, M // 2)
    table = both @ toeplitz
    high, low = split(table)
    main = np.concatenate([high[:, :HALF], low[:, :HALF]], 0)
    tail = np.concatenate([high[:, HALF:], low[:, HALF:]], 1)
    return main, tail


def lag_table():
    lags = np.arange(NLAG) - NLAG // 2
    bins = (BAND0 + np.arange(GROUPS)[:, None, None] + 32 * np.arange(4)[None, None, :])
    phase = 2.0 * math.pi * (((lags[:, None, None, None] + M) * bins[None]) % M) / M
    both = np.concatenate([np.cos(phase), -np.sin(phase)], 2).reshape(NLAG, 2 * FB)
    rounded = both.astype(np.float32).astype(ml_dtypes.bfloat16).astype(np.float32)
    return (rounded / 64.0).astype(ml_dtypes.bfloat16)


def spread_table():
    table = np.zeros((CH, 2, 4, 2, CH), np.float32)
    for c in range(CH):
        for o in range(2):
            table[c, o, :, o, c] = 1.0
    return table.reshape(CH * 8, 2 * CH).astype(ml_dtypes.bfloat16)


CHUNKS = 16
PART = 32
LENGTH = FRAMES * HALF
LAST = 16


def lags(lag, cross, which, target):
    for j in range(LAST):
        result = jnp.dot(lag[...], cross[which * LAST + j], preferred_element_type=F32)
        for d in range(2):
            flat = target.at[d].reshape(NLAG * LAST, CH)
            flat[pl.ds(j, NLAG, stride=LAST), :] = result[:, d * CH : (d + 1) * CH]


def exchange_kernel(record_ref, quality_ref, main_hbm, tail_hbm, spread_hbm, lag_hbm, near_ref, far_ref,
                    rec, main, tail, spread, lag, held, white, turned, got, left,
                    send_sem, recv_sem, rec_sem, table_sem, halo_sem):
    tables = [
        pltpu.make_async_copy(source, target, table_sem.at[i])
        for i, (source, target) in enumerate(
            [(main_hbm, main), (tail_hbm, tail), (spread_hbm, spread), (lag_hbm, lag)])
    ]

    def piece(i):
        at = pl.ds(pl.multiple_of(i * 2 * HALF, 2 * HALF), 2 * HALF)
        return pltpu.make_async_copy(record_ref.at[:, at], rec.at[:, at], rec_sem.at[i])

    piece(0).start()
    tables[0].start()
    tables[1].start()
    for i in range(1, FRAMES // 2):
        piece(i).start()
    tables[2].start()
    tables[3].start()

    me = lax.axis_index("blk")
    count = lax.axis_size("blk")
    ahead = lax.rem(me + 2, count)
    behind = lax.rem(me + count - 2, count)
    parity = lax.rem(me, 2)
    beside = me + 1 - 2 * parity
    segment = lax.axis_index("pre")
    segments = lax.axis_size("pre")
    sooner = lax.rem(segment + segments - 1, segments)
    later = lax.rem(segment + 1, segments)
    barrier = pltpu.get_barrier_semaphore()
    for other in (ahead, behind, beside):
        pl.semaphore_signal(barrier, inc=1, device_id={"blk": other}, device_id_type=pl.DeviceIdType.MESH)
    for other in (sooner, later):
        pl.semaphore_signal(barrier, inc=1, device_id={"pre": other}, device_id_type=pl.DeviceIdType.MESH)
    pl.semaphore_wait(barrier, 5)

    halo = pltpu.make_async_remote_copy(
        src_ref=record_ref.at[:, pl.ds(0, HALO)],
        dst_ref=rec.at[:, pl.ds(LENGTH, HALO)],
        send_sem=halo_sem.at[0],
        recv_sem=halo_sem.at[1],
        device_id={"pre": sooner},
        device_id_type=pl.DeviceIdType.MESH,
    )

    @pl.when(segment > 0)
    def _():
        halo.start()

    @pl.when(segment == segments - 1)
    def _():
        rec[:, LENGTH:] = jnp.zeros((CH, HALO), BF)

    def view(ref, half, which):
        if half == 0:
            return ref.at[:, pl.ds(pl.multiple_of(which * 16, 16), 16), :]
        return ref.at[pl.ds(which * 4, 4), pl.ds(128, 128), :]

    def copy(half, which, source, target, slot, device):
        return pltpu.make_async_remote_copy(
            src_ref=view(white if source == 0 else got.at[source - 1], half, which),
            dst_ref=view(got.at[target - 1], half, which),
            send_sem=send_sem.at[slot, half * 8 + which],
            recv_sem=recv_sem.at[target - 1, half * 8 + which],
            device_id={"blk": device},
            device_id_type=pl.DeviceIdType.MESH,
        )

    def arrived(half, which, source):
        copy(half, which, 0, source, 0, beside).wait_recv()

    def on(condition):
        return lambda body: pl.when(condition)(body)

    def offer(half, which):
        @on(parity == 0)
        def _():
            copy(half, which, 0, 1, 0, beside).start()

            @on(lax.rem(which, 2) == 0)
            def _():
                copy(half, which, 0, 2, 1, ahead).start()

        @on(parity == 1)
        def _():
            copy(half, which, 0, 2, 0, ahead).start()

    def relay(half, which):
        @on(parity == 0)
        def _():
            arrived(half, which, 1)
            copy(half, which, 1, 3, 2, ahead).start()

            @on(lax.rem(which, 2) == 0)
            def _():
                arrived(half, which, 2)
                copy(half, which, 2, 3, 3, beside).start()

        @on(parity == 1)
        def _():
            arrived(half, which, 2)
            copy(half, which, 2, 1, 1, beside).start()
            arrived(half, which, 1)

            @on(lax.rem(which, 2) == 1)
            def _():
                copy(half, which, 1, 3, 2, ahead).start()

    def finish(half, which):
        arrived(half, which, 3)

        @on(lax.rem(which, 2) == 1)
        def _():
            @on(parity == 0)
            def _():
                arrived(half, which, 2)

            @on(parity == 1)
            def _():
                copy(half, which, 3, 2, 3, beside).start()

    def transform(raw, after):
        both = lax.dot_general(main[...], raw, NT, preferred_element_type=F32)
        ends = jnp.concatenate([after, after], 1)
        return (both[:ROWS] + both[ROWS:]) + lax.dot_general(
            tail[...], ends, NT, preferred_element_type=F32)

    piece(0).wait()
    tables[0].wait()
    tables[1].wait()
    held[...] = transform(rec[:, :HALF], rec[:, HALF : HALF + 128]).reshape(GROUPS + 2, 8, CH)
    keep = quality_ref[...].astype(F32).reshape(1, 1, CH)

    def frames(step):
        start = pl.multiple_of(step * 2 * HALF + HALF, HALF)
        one = pl.ds(start, HALF)
        two = pl.ds(pl.multiple_of(start + HALF, HALF), HALF)
        raw = jnp.concatenate([rec[:, one], rec[:, two]], 0)
        after = jnp.concatenate([
            rec[:, pl.ds(pl.multiple_of(start + HALF, HALF), 128)],
            rec[:, pl.ds(pl.multiple_of(start + 2 * HALF, HALF), 128)]], 0)
        pair = transform(raw, after)
        zero = held[...]
        first = pair[:, :CH].reshape(GROUPS + 2, 8, CH)
        second = pair[:, CH:].reshape(GROUPS + 2, 8, CH)
        held[...] = second
        group = lax.broadcasted_iota(jnp.int32, (GROUPS, 8, CH), 0)
        odd = (group % 2) == 1
        row = lax.broadcasted_iota(jnp.int32, (GROUPS, 8, CH), 1)

        def whiten(front, back):
            side = 0.25 * (front[:GROUPS] + front[2:])
            spec = 0.5 * front[1 : GROUPS + 1] - side
            other = 0.5 * back[1 : GROUPS + 1] + 0.25 * (back[:GROUPS] + back[2:])
            spec = spec + jnp.where(odd, -other, other)
            square = spec * spec
            level = jnp.sum(jnp.sum(square, 0), 0, keepdims=True).reshape(1, 1, CH) * (1.0 / FB)
            power = square + pltpu.roll(square, 4, 1)
            plain = spec * lax.rsqrt(power + (0.1 * level + 1e-06)) * keep
            swapped = pltpu.roll(plain, 4, 1)
            return plain, jnp.where(row < 4, swapped, -swapped)

        w0, t0 = whiten(zero, first)
        w1, t1 = whiten(first, second)
        at = pl.ds(pl.multiple_of(step * 16, 16), 16)
        white[:, at, :] = jnp.concatenate([w0, w1], 1).astype(BF)
        turned[:, at, :] = jnp.concatenate([t0, t1], 1).astype(BF)

    @pl.loop(0, 8)
    def _(step):
        piece(step + 1).wait()
        frames(step)
        offer(0, step)

    @pl.loop(8, FRAMES // 2)
    def _(step):
        @on(step < FRAMES // 2 - 1)
        def _():
            piece(step + 1).wait()

        @on(jnp.logical_and(step == FRAMES // 2 - 1, segment < segments - 1))
        def _():
            halo.wait_recv()

        frames(step)

        @on(lax.rem(step, 3) == 0)
        def _():
            relay(0, lax.div(step, 3) - 3)

    @pl.loop(0, 8)
    def _(which):
        offer(1, which)

    tables[2].wait()
    tables[3].wait()
    rows = lax.broadcasted_iota(jnp.int32, (PART * 8, 256), 0)
    cols = lax.broadcasted_iota(jnp.int32, (PART * 8, 256), 1)
    diagonal = (rows % 4) == (cols % 4)

    @pl.loop(3, 8)
    def _(which):
        relay(0, which)

        @on(which < 7)
        def _():
            @pl.loop(0, 8)
            def _(j):
                group = (which - 3) * 8 + j
                own = jnp.concatenate([white[group], turned[group]], 1)
                for part in range(CH // PART):
                    lines = pl.ds(part * PART * 8, PART * 8)
                    table = lax.dot_general(spread[lines, :], own, NT, preferred_element_type=F32)
                    left[group, lines, :] = jnp.where(diagonal, table, 0.0).astype(BF)

    def products(pair, one, two, store):
        for part in range(CH // PART):
            lines = pl.ds(part * PART * 8, PART * 8)
            pieces = []
            for j in range(2):
                group = 2 * pair + j
                right = jnp.concatenate([one[group], two[group]], 1)
                pieces.append(
                    jnp.dot(left[group, lines, :], right, preferred_element_type=F32).reshape(PART, 8, 2 * CH))
            store(part, jnp.concatenate(pieces, 1).astype(BF))

    def fill(which, one, two):
        @pl.loop(0, 2)
        def _(j):
            pair = which * 2 + j

            def store(part, value):
                far_ref[pl.ds(part * PART, PART), pl.ds(pl.multiple_of(pair * 16, 16), 16), :] = value

            products(pair, one, two, store)

    @pl.loop(0, 8)
    def _(which):
        relay(1, which)
        fill(which, white, got.at[0])

    @pl.loop(0, 8)
    def _(which):
        finish(0, which)
        lags(lag, far_ref, which, near_ref.at[which])

    @pl.loop(0, 8)
    def _(which):
        finish(1, which)
        fill(which, got.at[1], got.at[2])

    @on(segment > 0)
    def _():
        halo.wait_send()

    for half in range(2):
        @pl.loop(0, 8)
        def _(which):
            copy(half, which, 0, 1, 0, beside).wait_send()

            @on(parity == 0)
            def _():
                copy(half, which, 1, 3, 2, ahead).wait_send()

                @on(lax.rem(which, 2) == 0)
                def _():
                    copy(half, which, 0, 2, 1, ahead).wait_send()
                    copy(half, which, 2, 3, 3, beside).wait_send()

            @on(parity == 1)
            def _():
                copy(half, which, 2, 1, 1, beside).wait_send()

                @on(lax.rem(which, 2) == 1)
                def _():
                    copy(half, which, 1, 3, 2, ahead).wait_send()
                    copy(half, which, 3, 2, 3, beside).wait_send()


def exchange(record, quality):
    tables = [jnp.asarray(t) for t in half_tables() + (spread_table(), lag_table())]
    anywhere = pl.BlockSpec(memory_space=pl.ANY)
    return pl.pallas_call(
        exchange_kernel,
        out_shape=(
            pltpu.VMEM((CH // LAST, 2, NLAG, LAST, CH), F32),
            pltpu.VMEM((CH, 2 * FB, 2 * CH), BF),
        ),
        in_specs=[anywhere, pl.BlockSpec(memory_space=pltpu.VMEM)] + [anywhere] * 4,
        out_specs=(pl.BlockSpec(memory_space=pltpu.VMEM),) * 2,
        scratch_shapes=[
            pltpu.VMEM((CH, LENGTH + HALO), BF),
            pltpu.VMEM((2 * ROWS, HALF), BF),
            pltpu.VMEM((ROWS, 256), BF),
            pltpu.VMEM((CH * 8, 256), BF),
            pltpu.VMEM((NLAG, 2 * FB), BF),
            pltpu.VMEM((GROUPS + 2, 8, CH), F32),
            pltpu.VMEM((GROUPS, 256, CH), BF),
            pltpu.VMEM((GROUPS, 256, CH), BF),
            pltpu.VMEM((3, GROUPS, 256, CH), BF),
            pltpu.VMEM((GROUPS, CH * 8, 256), BF),
            pltpu.SemaphoreType.DMA((4, CHUNKS)),
            pltpu.SemaphoreType.DMA((3, CHUNKS)),
            pltpu.SemaphoreType.DMA((FRAMES // 2,)),
            pltpu.SemaphoreType.DMA((4,)),
            pltpu.SemaphoreType.DMA((2,)),
        ],
        compiler_params=pltpu.CompilerParams(
            collective_id=0, has_side_effects=True, vmem_limit_bytes=38 * 2**20),
        name="exchange",
    )(record, quality.reshape(1, CH), *tables)


def last_kernel(lag, near, far, out_ref, staged, near_sem, far_sem):
    def store_near(which):
        at = pl.ds(pl.multiple_of(which * LAST, LAST), LAST)
        return pltpu.make_async_copy(near.at[which], out_ref.at[pl.ds(0, 2), :, at, :], near_sem.at[which])

    def store_far(which):
        at = pl.ds(pl.multiple_of(which * LAST, LAST), LAST)
        buffer = lax.rem(which, 2)
        return pltpu.make_async_copy(staged.at[buffer], out_ref.at[pl.ds(2, 2), :, at, :], far_sem.at[buffer])

    steps = CH // LAST

    @pl.loop(0, steps)
    def _(which):
        store_near(which).start()

        @pl.when(which > 1)
        def _():
            store_far(which - 2).wait()

        lags(lag, far, which, staged.at[lax.rem(which, 2)])
        store_far(which).start()

    for which in (steps - 2, steps - 1):
        store_far(which).wait()

    @pl.loop(0, steps)
    def _(which):
        store_near(which).wait()


def last(near, far):
    inside = pl.BlockSpec(memory_space=pltpu.VMEM)
    return pl.pallas_call(
        last_kernel,
        out_shape=jax.ShapeDtypeStruct((4, NLAG, CH, CH), F32),
        in_specs=[inside] * 3,
        out_specs=pl.BlockSpec(memory_space=pl.ANY),
        scratch_shapes=[
            pltpu.VMEM((2, 2, NLAG, LAST, CH), F32),
            pltpu.SemaphoreType.DMA((CH // LAST,)),
            pltpu.SemaphoreType.DMA((2,)),
        ],
        compiler_params=pltpu.CompilerParams(vmem_limit_bytes=8 * 2**20),
        name="last",
    )(jnp.asarray(lag_table()), near, far)


def shards(record, quality):
    return last(*exchange(record, quality))[None]


def solution(mesh):
    placed = (P("blk", "pre"), P("blk"))
    return jax.shard_map(
        shards,
        mesh=mesh,
        in_specs=placed,
        out_specs=P("pre", None, None, "blk", None),
        check_vma=False,
    )
```

```python
import math

import jax
import jax.numpy as jnp
import ml_dtypes
import numpy as np
from jax import lax
from jax.experimental import pallas as pl
from jax.experimental.pallas import tpu as pltpu
from jax.sharding import PartitionSpec as P

M = 512
R = 4
KT = 16
FB = 128
NLAG = 64
BAND0 = 16
CH = 128
HALF = 1024
FRAMES = 32
GROUPS = 32
ROWS = (GROUPS + 2) * 8
HALO = HALF + 128
NT = (((1,), (1,)), ((), ()))
BF = jnp.bfloat16
F32 = jnp.float32


def filter_taps():
    index = np.arange(KT, dtype=np.float32)
    centre = np.float32((KT - 1) / 2.0)
    shaped = np.sinc((index - centre) / np.float32(R)) * (
        0.54 - 0.46 * np.cos(2.0 * math.pi * index / (KT - 1))
    )
    return (shaped / np.sum(shaped)).astype(np.float32).astype(ml_dtypes.bfloat16)


def split(table):
    high = table.astype(np.float32).astype(ml_dtypes.bfloat16)
    low = (table - high.astype(np.float64)).astype(np.float32).astype(ml_dtypes.bfloat16)
    return high, low


def half_tables():
    taps = filter_taps().astype(np.float64)
    toeplitz = np.zeros((M // 2, HALF + 128))
    for m in range(M // 2):
        toeplitz[m, R * m : R * m + KT] = taps
    group = np.arange(-1, GROUPS + 1)
    bins = BAND0 + group[:, None] + 32 * np.arange(4)[None, :]
    phase = 2.0 * math.pi * ((bins[:, :, None] * np.arange(M // 2)) % M) / M
    both = np.stack([np.cos(phase), -np.sin(phase)], 1).reshape(ROWS, M // 2)
    table = both @ toeplitz
    high, low = split(table)
    main = np.concatenate([high[:, :HALF], low[:, :HALF]], 0)
    tail = np.concatenate([high[:, HALF:], low[:, HALF:]], 1)
    return main, tail


def lag_table():
    lags = np.arange(NLAG) - NLAG // 2
    bins = (BAND0 + np.arange(GROUPS)[:, None, None] + 32 * np.arange(4)[None, None, :])
    phase = 2.0 * math.pi * (((lags[:, None, None, None] + M) * bins[None]) % M) / M
    both = np.concatenate([np.cos(phase), -np.sin(phase)], 2).reshape(NLAG, 2 * FB)
    rounded = both.astype(np.float32).astype(ml_dtypes.bfloat16).astype(np.float32)
    return (rounded / 64.0).astype(ml_dtypes.bfloat16)


def spread_table():
    table = np.zeros((CH, 2, 4, 2, CH), np.float32)
    for c in range(CH):
        for o in range(2):
            table[c, o, :, o, c] = 1.0
    return table.reshape(CH * 8, 2 * CH).astype(ml_dtypes.bfloat16)


CHUNKS = 16
PART = 32
LENGTH = FRAMES * HALF
LAST = 16


KINDS = [5, 6, 3, 5, 6, 2, 2, 2, 7, 3, 4, 2, 3, 3, 7, 4]
OWN = {
    0: {2: [("y", 1), ("z", 2)], 3: [("y", 1)], 4: [("y", 1)], 5: [("d", 4), ("y", 1)],
        6: [("y", 1), ("z", 2)], 7: [("d", 4), ("y", 1)]},
    1: {kind: [("z", 2)] for kind in range(2, 8)},
}
ONWARD = {
    0: {
        2: {1: ("z", 3), 2: ("y", 3)},
        3: {1: ("z", 3)},
        4: {1: ("z", 3)},
        5: {1: ("z", 3), 2: ("y", 3), 4: ("d", 5), 5: ("e", 2)},
        6: {1: ("z", 3)},
        7: {1: ("z", 3), 4: ("d", 5), 5: ("e", 2)},
    },
    1: {
        2: {2: ("y", 1)},
        3: {2: ("y", 1), 1: ("z", 3), 3: ("y", 2)},
        4: {2: ("y", 1), 1: ("d", 4), 4: ("d", 5), 5: ("e", 3), 3: ("y", 2)},
        5: {2: ("y", 1)},
        6: {2: ("y", 1), 1: ("d", 4), 4: ("d", 5), 5: ("e", 3)},
        7: {2: ("y", 1), 1: ("z", 3)},
    },
}
ARRIVALS = (
    [
        [],
        [],
        [],
        [],
        [],
        [],
        [(4, 0)],
        [(2, 1)],
        [],
        [(4, 3)],
        [(2, 4)],
        [(1, 0)],
        [(5, 0)],
        [(2, 5)],
        [],
        [(1, 1), (5, 3)],
        [(2, 6), (1, 2)],
        [(2, 0)],
        [],
        [(2, 7)],
        [],
        [(1, 3)],
        [(2, 3)],
        [],
        [(3, 0)],
        [],
        [(1, 4)],
        [(4, 8)],
        [],
        [(3, 1)],
        [],
        [(1, 5)],
        [(4, 14), (2, 11), (1, 6), (5, 8), (3, 2), (1, 7), (5, 14), (3, 3), (2, 2), (2, 8), (3, 4), (1, 8)],
        [(2, 14), (3, 5), (1, 9)],
        [(3, 6), (1, 10)],
        [(3, 7), (1, 11)],
        [(3, 8), (1, 12)],
        [(3, 9), (1, 13)],
        [(3, 10), (1, 14)],
        [(3, 11), (1, 15)],
        [],
        [(3, 12)],
        [],
        [(2, 10)],
        [(3, 13)],
        [],
        [(2, 9)],
        [],
        [(3, 14)],
        [(2, 12)],
        [(3, 15)],
        [],
        [(2, 13)],
        [],
        [(2, 15)],
        [],
        [],
    ],
    [
        [],
        [],
        [],
        [],
        [],
        [],
        [(1, 0), (2, 0)],
        [],
        [],
        [(1, 1), (2, 1)],
        [],
        [],
        [(1, 2), (2, 2)],
        [],
        [],
        [(4, 1), (1, 3), (2, 3)],
        [],
        [(1, 4), (2, 4)],
        [],
        [],
        [],
        [(5, 1)],
        [(1, 5), (2, 5)],
        [],
        [],
        [],
        [(4, 4)],
        [(1, 6), (2, 6)],
        [],
        [],
        [],
        [(3, 1)],
        [(1, 7), (2, 7), (5, 4), (3, 2), (3, 5), (1, 8), (2, 8)],
        [(3, 4), (1, 9), (2, 9)],
        [(1, 10), (2, 10)],
        [(1, 11), (2, 11)],
        [(4, 10), (1, 12), (2, 12)],
        [(1, 13), (2, 13)],
        [(5, 10), (1, 14), (2, 14)],
        [(1, 15), (2, 15)],
        [(3, 10)],
        [],
        [(3, 6), (3, 8)],
        [],
        [],
        [(4, 15)],
        [(3, 0), (3, 9)],
        [],
        [(3, 7), (3, 12), (5, 15), (3, 3), (3, 13)],
        [],
        [],
        [(3, 11), (3, 14), (3, 15)],
        [],
        [],
        [],
        [],
        [],
    ],
)
PASSING = {0: (5, 7), 1: (4, 6)}


def sends_of(parity, chunk):
    kind = KINDS[chunk]
    return [(0,) + way for way in OWN[parity][kind]] + [
        (buffer,) + way for buffer, way in sorted(ONWARD[parity][kind].items())]


def passing_place(parity, chunk):
    first = chunk - chunk % 8
    return sum(KINDS[c] in PASSING[parity] for c in range(first, chunk))


def lags(lag, cross, which, target):
    for j in range(LAST):
        result = jnp.dot(lag[...], cross[which * LAST + j], preferred_element_type=F32)
        for d in range(2):
            flat = target.at[d].reshape(NLAG * LAST, CH)
            flat[pl.ds(j, NLAG, stride=LAST), :] = result[:, d * CH : (d + 1) * CH]


def exchange_kernel(record_ref, quality_ref, main_hbm, tail_hbm, spread_hbm, lag_hbm, near_ref, far_ref,
                    rec, main, tail, spread, lag, held, white, turned, got, early, late, left,
                    send_sem, recv_sem, rec_sem, table_sem, halo_sem):
    tables = [
        pltpu.make_async_copy(source, target, table_sem.at[i])
        for i, (source, target) in enumerate(
            [(main_hbm, main), (tail_hbm, tail), (spread_hbm, spread), (lag_hbm, lag)])
    ]

    def piece(i):
        at = pl.ds(pl.multiple_of(i * 2 * HALF, 2 * HALF), 2 * HALF)
        return pltpu.make_async_copy(record_ref.at[:, at], rec.at[:, at], rec_sem.at[i])

    piece(0).start()
    tables[0].start()
    tables[1].start()
    for i in range(1, FRAMES // 2):
        piece(i).start()
    tables[2].start()
    tables[3].start()

    me = lax.axis_index("blk")
    count = lax.axis_size("blk")
    ahead = lax.rem(me + 2, count)
    behind = lax.rem(me + count - 2, count)
    parity = lax.rem(me, 2)
    beside = me + 1 - 2 * parity
    column = lax.div(me, 2)
    x, z = lax.div(column, 4), lax.rem(column, 4)
    columns = lax.div(count, 2)
    below = 2 * (x * 4 + lax.rem(z + 3, 4)) + parity
    above = 2 * (x * 4 + lax.rem(z + 1, 4)) + parity
    target = 2 * lax.rem(x * 4 + lax.rem(z + 2, 4) + 1, columns) + parity
    origin = lax.rem(column + columns - 1, columns)
    source_of_me = 2 * (lax.div(origin, 4) * 4 + lax.rem(lax.rem(origin, 4) + 2, 4)) + parity
    segment = lax.axis_index("pre")
    segments = lax.axis_size("pre")
    sooner = lax.rem(segment + segments - 1, segments)
    later = lax.rem(segment + 1, segments)
    barrier = pltpu.get_barrier_semaphore()
    for other in (ahead, behind, beside, below, above, target, source_of_me):
        pl.semaphore_signal(barrier, inc=1, device_id={"blk": other}, device_id_type=pl.DeviceIdType.MESH)
    for other in (sooner, later):
        pl.semaphore_signal(barrier, inc=1, device_id={"pre": other}, device_id_type=pl.DeviceIdType.MESH)
    pl.semaphore_wait(barrier, 9)

    halo = pltpu.make_async_remote_copy(
        src_ref=record_ref.at[:, pl.ds(0, HALO)],
        dst_ref=rec.at[:, pl.ds(LENGTH, HALO)],
        send_sem=halo_sem.at[0],
        recv_sem=halo_sem.at[1],
        device_id={"pre": sooner},
        device_id_type=pl.DeviceIdType.MESH,
    )

    @pl.when(segment > 0)
    def _():
        halo.start()

    @pl.when(segment == segments - 1)
    def _():
        rec[:, LENGTH:] = jnp.zeros((CH, HALO), BF)

    devices = {"y": beside, "z": ahead, "d": below, "e": target}

    def view(buffer, side, chunk):
        half, which = divmod(chunk, 8)
        if buffer > 3:
            return (early, late)[half].at[buffer - 4, passing_place(side, chunk)]
        ref = white if buffer == 0 else got.at[buffer - 1]
        if half == 0:
            return ref.at[:, pl.ds(which * 16, 16), :]
        return ref.at[pl.ds(which * 4, 4), pl.ds(128, 128), :]

    def copy(side, chunk, buffer, way, there):
        slot = sends_of(side, chunk).index((buffer, way, there))
        return pltpu.make_async_remote_copy(
            src_ref=view(buffer, side, chunk),
            dst_ref=view(there, side, chunk),
            send_sem=send_sem.at[slot, chunk],
            recv_sem=recv_sem.at[there - 1, chunk],
            device_id={"blk": devices[way]},
            device_id_type=pl.DeviceIdType.MESH,
        )

    def landed(side, chunk, buffer):
        return pltpu.make_async_remote_copy(
            src_ref=view(buffer, side, chunk),
            dst_ref=view(buffer, side, chunk),
            send_sem=send_sem.at[0, chunk],
            recv_sem=recv_sem.at[buffer - 1, chunk],
            device_id={"blk": beside},
            device_id_type=pl.DeviceIdType.MESH,
        )

    def on(condition):
        return lambda body: pl.when(condition)(body)

    def offer(side, chunk):
        for way, there in OWN[side][KINDS[chunk]]:
            copy(side, chunk, 0, way, there).start()

    def each_side(body):
        for side in range(2):
            @on(parity == side)
            def _():
                body(side)

    def visit(piece_at, step, steps):
        def body(side):
            for i in range(steps):
                if ARRIVALS[side][piece_at + i]:
                    @on(step == i)
                    def _():
                        for buffer, chunk in ARRIVALS[side][piece_at + i]:
                            landed(side, chunk, buffer).wait_recv()
                            onward = ONWARD[side][KINDS[chunk]].get(buffer)
                            if onward:
                                copy(side, chunk, buffer, *onward).start()

        each_side(body)

    def transform(raw, after):
        both = lax.dot_general(main[...], raw, NT, preferred_element_type=F32)
        ends = jnp.concatenate([after, after], 1)
        return (both[:ROWS] + both[ROWS:]) + lax.dot_general(
            tail[...], ends, NT, preferred_element_type=F32)

    piece(0).wait()
    tables[0].wait()
    tables[1].wait()
    held[...] = transform(rec[:, :HALF], rec[:, HALF : HALF + 128]).reshape(GROUPS + 2, 8, CH)
    keep = quality_ref[...].astype(F32).reshape(1, 1, CH)

    def frames(step):
        start = pl.multiple_of(step * 2 * HALF + HALF, HALF)
        one = pl.ds(start, HALF)
        two = pl.ds(pl.multiple_of(start + HALF, HALF), HALF)
        raw = jnp.concatenate([rec[:, one], rec[:, two]], 0)
        after = jnp.concatenate([
            rec[:, pl.ds(pl.multiple_of(start + HALF, HALF), 128)],
            rec[:, pl.ds(pl.multiple_of(start + 2 * HALF, HALF), 128)]], 0)
        pair = transform(raw, after)
        zero = held[...]
        first = pair[:, :CH].reshape(GROUPS + 2, 8, CH)
        second = pair[:, CH:].reshape(GROUPS + 2, 8, CH)
        held[...] = second
        group = lax.broadcasted_iota(jnp.int32, (GROUPS, 8, CH), 0)
        odd = (group % 2) == 1
        row = lax.broadcasted_iota(jnp.int32, (GROUPS, 8, CH), 1)

        def whiten(front, back):
            side = 0.25 * (front[:GROUPS] + front[2:])
            spec = 0.5 * front[1 : GROUPS + 1] - side
            other = 0.5 * back[1 : GROUPS + 1] + 0.25 * (back[:GROUPS] + back[2:])
            spec = spec + jnp.where(odd, -other, other)
            square = spec * spec
            level = jnp.sum(jnp.sum(square, 0), 0, keepdims=True).reshape(1, 1, CH) * (1.0 / FB)
            power = square + pltpu.roll(square, 4, 1)
            plain = spec * lax.rsqrt(power + (0.1 * level + 1e-06)) * keep
            swapped = pltpu.roll(plain, 4, 1)
            return plain, jnp.where(row < 4, swapped, -swapped)

        w0, t0 = whiten(zero, first)
        w1, t1 = whiten(first, second)
        at = pl.ds(pl.multiple_of(step * 16, 16), 16)
        white[:, at, :] = jnp.concatenate([w0, w1], 1).astype(BF)
        turned[:, at, :] = jnp.concatenate([t0, t1], 1).astype(BF)

    @pl.loop(0, FRAMES // 2)
    def _(step):
        visit(0, step, 16)

        @on(step < FRAMES // 2 - 1)
        def _():
            piece(step + 1).wait()

        @on(jnp.logical_and(step == FRAMES // 2 - 1, segment < segments - 1))
        def _():
            halo.wait_recv()

        frames(step)

        def body(side):
            for i in range(8):
                @on(step == i)
                def _():
                    offer(side, i)

        each_side(body)

    def rest(side):
        for chunk in range(8, CHUNKS):
            offer(side, chunk)

    each_side(rest)

    tables[2].wait()
    tables[3].wait()
    rows = lax.broadcasted_iota(jnp.int32, (PART * 8, 256), 0)
    cols = lax.broadcasted_iota(jnp.int32, (PART * 8, 256), 1)
    diagonal = (rows % 4) == (cols % 4)

    @pl.loop(0, GROUPS // 2)
    def _(step):
        visit(16, step, 16)
        for j in range(2):
            group = step * 2 + j
            own = jnp.concatenate([white[group], turned[group]], 1)
            for part in range(CH // PART):
                lines = pl.ds(part * PART * 8, PART * 8)
                table = lax.dot_general(spread[lines, :], own, NT, preferred_element_type=F32)
                left[group, lines, :] = jnp.where(diagonal, table, 0.0).astype(BF)

    def products(pair, one, two, store):
        for part in range(CH // PART):
            lines = pl.ds(part * PART * 8, PART * 8)
            pieces = []
            for j in range(2):
                group = 2 * pair + j
                right = jnp.concatenate([one[group], two[group]], 1)
                pieces.append(
                    jnp.dot(left[group, lines, :], right, preferred_element_type=F32).reshape(PART, 8, 2 * CH))
            store(part, jnp.concatenate(pieces, 1).astype(BF))

    def fill(which, one, two):
        @pl.loop(0, 2)
        def _(j):
            pair = which * 2 + j

            def store(part, value):
                far_ref[pl.ds(part * PART, PART), pl.ds(pl.multiple_of(pair * 16, 16), 16), :] = value

            products(pair, one, two, store)

    @pl.loop(0, 8)
    def _(which):
        visit(32, which, 8)
        fill(which, white, got.at[0])

    @pl.loop(0, 8)
    def _(which):
        visit(40, which, 8)
        lags(lag, far_ref, which, near_ref.at[which])

    @pl.loop(0, 8)
    def _(which):
        visit(48, which, 8)
        fill(which, got.at[1], got.at[2])

    visit(56, 0, 1)

    @on(segment > 0)
    def _():
        halo.wait_send()

    def sent(side):
        for chunk in range(CHUNKS):
            for buffer, way, there in sends_of(side, chunk):
                copy(side, chunk, buffer, way, there).wait_send()

    each_side(sent)


def exchange(record, quality):
    tables = [jnp.asarray(t) for t in half_tables() + (spread_table(), lag_table())]
    anywhere = pl.BlockSpec(memory_space=pl.ANY)
    return pl.pallas_call(
        exchange_kernel,
        out_shape=(
            pltpu.VMEM((CH // LAST, 2, NLAG, LAST, CH), F32),
            pltpu.VMEM((CH, 2 * FB, 2 * CH), BF),
        ),
        in_specs=[anywhere, pl.BlockSpec(memory_space=pltpu.VMEM)] + [anywhere] * 4,
        out_specs=(pl.BlockSpec(memory_space=pltpu.VMEM),) * 2,
        scratch_shapes=[
            pltpu.VMEM((CH, LENGTH + HALO), BF),
            pltpu.VMEM((2 * ROWS, HALF), BF),
            pltpu.VMEM((ROWS, 256), BF),
            pltpu.VMEM((CH * 8, 256), BF),
            pltpu.VMEM((NLAG, 2 * FB), BF),
            pltpu.VMEM((GROUPS + 2, 8, CH), F32),
            pltpu.VMEM((GROUPS, 256, CH), BF),
            pltpu.VMEM((GROUPS, 256, CH), BF),
            pltpu.VMEM((3, GROUPS, 256, CH), BF),
            pltpu.VMEM((2, 2, GROUPS, 16, CH), BF),
            pltpu.VMEM((2, 2, 4, 128, CH), BF),
            pltpu.VMEM((GROUPS, CH * 8, 256), BF),
            pltpu.SemaphoreType.DMA((6, CHUNKS)),
            pltpu.SemaphoreType.DMA((5, CHUNKS)),
            pltpu.SemaphoreType.DMA((FRAMES // 2,)),
            pltpu.SemaphoreType.DMA((4,)),
            pltpu.SemaphoreType.DMA((2,)),
        ],
        compiler_params=pltpu.CompilerParams(
            collective_id=0, has_side_effects=True, vmem_limit_bytes=39 * 2**20),
        name="exchange",
    )(record, quality.reshape(1, CH), *tables)


def last_kernel(lag, near, far, out_ref, staged, near_sem, far_sem):
    def store_near(which):
        at = pl.ds(pl.multiple_of(which * LAST, LAST), LAST)
        return pltpu.make_async_copy(near.at[which], out_ref.at[pl.ds(0, 2), :, at, :], near_sem.at[which])

    def store_far(which):
        at = pl.ds(pl.multiple_of(which * LAST, LAST), LAST)
        buffer = lax.rem(which, 2)
        return pltpu.make_async_copy(staged.at[buffer], out_ref.at[pl.ds(2, 2), :, at, :], far_sem.at[buffer])

    steps = CH // LAST

    @pl.loop(0, steps)
    def _(which):
        store_near(which).start()

        @pl.when(which > 1)
        def _():
            store_far(which - 2).wait()

        lags(lag, far, which, staged.at[lax.rem(which, 2)])
        store_far(which).start()

    for which in (steps - 2, steps - 1):
        store_far(which).wait()

    @pl.loop(0, steps)
    def _(which):
        store_near(which).wait()


def last(near, far):
    inside = pl.BlockSpec(memory_space=pltpu.VMEM)
    return pl.pallas_call(
        last_kernel,
        out_shape=jax.ShapeDtypeStruct((4, NLAG, CH, CH), F32),
        in_specs=[inside] * 3,
        out_specs=pl.BlockSpec(memory_space=pl.ANY),
        scratch_shapes=[
            pltpu.VMEM((2, 2, NLAG, LAST, CH), F32),
            pltpu.SemaphoreType.DMA((CH // LAST,)),
            pltpu.SemaphoreType.DMA((2,)),
        ],
        compiler_params=pltpu.CompilerParams(vmem_limit_bytes=8 * 2**20),
        name="last",
    )(jnp.asarray(lag_table()), near, far)


def shards(record, quality):
    return last(*exchange(record, quality))[None]


def solution(mesh):
    placed = (P("blk", "pre"), P("blk"))
    return jax.shard_map(
        shards,
        mesh=mesh,
        in_specs=placed,
        out_specs=P("pre", None, None, "blk", None),
        check_vma=False,
    )
```

```python
import math

import jax
import jax.numpy as jnp
import ml_dtypes
import numpy as np
from jax import lax
from jax.experimental import pallas as pl
from jax.experimental.pallas import tpu as pltpu
from jax.sharding import PartitionSpec as P

M = 512
R = 4
KT = 16
FB = 128
NLAG = 64
BAND0 = 16
CH = 128
HALF = 1024
FRAMES = 32
GROUPS = 32
ROWS = (GROUPS + 2) * 8
HALO = HALF + 128
NT = (((1,), (1,)), ((), ()))
BF = jnp.bfloat16
F32 = jnp.float32


def filter_taps():
    index = np.arange(KT, dtype=np.float32)
    centre = np.float32((KT - 1) / 2.0)
    shaped = np.sinc((index - centre) / np.float32(R)) * (
        0.54 - 0.46 * np.cos(2.0 * math.pi * index / (KT - 1))
    )
    return (shaped / np.sum(shaped)).astype(np.float32).astype(ml_dtypes.bfloat16)


def split(table):
    high = table.astype(np.float32).astype(ml_dtypes.bfloat16)
    low = (table - high.astype(np.float64)).astype(np.float32).astype(ml_dtypes.bfloat16)
    return high, low


def half_tables():
    taps = filter_taps().astype(np.float64)
    toeplitz = np.zeros((M // 2, HALF + 128))
    for m in range(M // 2):
        toeplitz[m, R * m : R * m + KT] = taps
    group = np.arange(-1, GROUPS + 1)
    bins = BAND0 + group[:, None] + 32 * np.arange(4)[None, :]
    phase = 2.0 * math.pi * ((bins[:, :, None] * np.arange(M // 2)) % M) / M
    both = np.stack([np.cos(phase), -np.sin(phase)], 1).reshape(ROWS, M // 2)
    table = both @ toeplitz
    high, low = split(table)
    main = np.concatenate([high[:, :HALF], low[:, :HALF]], 0)
    tail = np.concatenate([high[:, HALF:], low[:, HALF:]], 1)
    return main, tail


def lag_table():
    lags = np.arange(NLAG) - NLAG // 2
    bins = (BAND0 + np.arange(GROUPS)[:, None, None] + 32 * np.arange(4)[None, None, :])
    phase = 2.0 * math.pi * (((lags[:, None, None, None] + M) * bins[None]) % M) / M
    both = np.concatenate([np.cos(phase), -np.sin(phase)], 2).reshape(NLAG, 2 * FB)
    rounded = both.astype(np.float32).astype(ml_dtypes.bfloat16).astype(np.float32)
    return (rounded / 64.0).astype(ml_dtypes.bfloat16)


def spread_table():
    table = np.zeros((CH, 2, 4, 2, CH), np.float32)
    for c in range(CH):
        for o in range(2):
            table[c, o, :, o, c] = 1.0
    return table.reshape(CH * 8, 2 * CH).astype(ml_dtypes.bfloat16)


CHUNKS = 16
PART = 32
LENGTH = FRAMES * HALF
LAST = 16


KINDS = [2, 5, 6, 6, 3, 7, 6, 7, 4, 4, 2, 2, 5, 3, 3, 7]
OWN = {
    0: {2: [("y", 1), ("z", 2)], 3: [("y", 1)], 4: [("y", 1)], 5: [("d", 4), ("y", 1)],
        6: [("y", 1), ("z", 2)], 7: [("d", 4), ("y", 1)]},
    1: {kind: [("z", 2)] for kind in range(2, 8)},
}
ONWARD = {
    0: {
        2: {1: ("z", 3), 2: ("y", 3)},
        3: {1: ("z", 3)},
        4: {1: ("z", 3)},
        5: {1: ("z", 3), 2: ("y", 3), 4: ("d", 5), 5: ("e", 2)},
        6: {1: ("z", 3)},
        7: {1: ("z", 3), 4: ("d", 5), 5: ("e", 2)},
    },
    1: {
        2: {2: ("y", 1)},
        3: {2: ("y", 1), 1: ("z", 3), 3: ("y", 2)},
        4: {2: ("y", 1), 1: ("d", 4), 4: ("d", 5), 5: ("e", 3), 3: ("y", 2)},
        5: {2: ("y", 1)},
        6: {2: ("y", 1), 1: ("d", 4), 4: ("d", 5), 5: ("e", 3)},
        7: {2: ("y", 1), 1: ("z", 3)},
    },
}
ARRIVALS = (
    [
        [],
        [],
        [],
        [],
        [],
        [],
        [(2, 0)],
        [(4, 1)],
        [],
        [(2, 2)],
        [],
        [(4, 5), (1, 0)],
        [(2, 3)],
        [],
        [(5, 1)],
        [(1, 1), (2, 6)],
        [(4, 7), (1, 2)],
        [(3, 0)],
        [],
        [],
        [],
        [(5, 5), (1, 3)],
        [(3, 1)],
        [],
        [],
        [],
        [(2, 1), (1, 4)],
        [(2, 10)],
        [],
        [],
        [],
        [(4, 12), (1, 5)],
        [(2, 11), (4, 15), (1, 6), (3, 2), (5, 7), (1, 7), (3, 3), (2, 5), (1, 8)],
        [(3, 4), (5, 12), (1, 9)],
        [(3, 5), (5, 15), (1, 10)],
        [(3, 6), (2, 7), (1, 11)],
        [(3, 7), (2, 12), (1, 12)],
        [(3, 8), (2, 15), (1, 13)],
        [(3, 9), (1, 14)],
        [(3, 10), (1, 15)],
        [(3, 11)],
        [],
        [],
        [(2, 4), (3, 12)],
        [],
        [],
        [(2, 8), (3, 13)],
        [],
        [],
        [(2, 9), (3, 14)],
        [],
        [],
        [(2, 13), (3, 15)],
        [],
        [(2, 14)],
        [],
        [],
    ],
    [
        [],
        [],
        [],
        [],
        [],
        [],
        [(1, 0), (2, 0)],
        [],
        [],
        [(1, 1), (2, 1)],
        [],
        [],
        [(1, 2), (2, 2)],
        [],
        [],
        [(1, 3), (2, 3)],
        [(4, 2)],
        [(1, 4), (2, 4)],
        [],
        [],
        [],
        [(4, 3)],
        [(1, 5), (2, 5)],
        [],
        [],
        [],
        [(5, 2)],
        [(2, 6), (3, 0)],
        [],
        [],
        [],
        [(5, 3)],
        [(1, 6), (2, 7), (3, 2), (1, 7), (2, 8), (3, 3), (1, 8), (2, 9)],
        [(4, 6), (1, 9), (2, 10)],
        [(4, 8), (1, 10), (2, 11)],
        [(5, 6), (1, 11), (2, 12)],
        [(4, 9), (1, 12), (2, 13)],
        [(5, 8), (1, 13), (2, 14)],
        [(3, 6), (1, 14), (2, 15)],
        [(5, 9), (1, 15), (3, 4)],
        [],
        [],
        [(3, 8), (3, 1), (3, 5)],
        [],
        [],
        [(3, 9)],
        [(3, 7), (3, 10)],
        [],
        [],
        [(3, 11), (3, 13)],
        [],
        [(3, 12), (3, 14)],
        [],
        [],
        [(3, 15)],
        [],
        [],
    ],
)
PASSING = {0: (5, 7), 1: (4, 6)}


def sends_of(parity, chunk):
    kind = KINDS[chunk]
    return [(0,) + way for way in OWN[parity][kind]] + [
        (buffer,) + way for buffer, way in sorted(ONWARD[parity][kind].items())]


def passing_place(parity, chunk):
    first = chunk - chunk % 8
    return sum(KINDS[c] in PASSING[parity] for c in range(first, chunk))


def lags(lag, cross, which, target):
    for j in range(LAST):
        result = jnp.dot(lag[...], cross[which * LAST + j], preferred_element_type=F32)
        for d in range(2):
            flat = target.at[d].reshape(NLAG * LAST, CH)
            flat[pl.ds(j, NLAG, stride=LAST), :] = result[:, d * CH : (d + 1) * CH]


def exchange_kernel(record_ref, quality_ref, main_hbm, tail_hbm, spread_hbm, lag_hbm, near_ref, far_ref,
                    rec, main, tail, spread, lag, held, white, turned, got, early, late, left,
                    send_sem, recv_sem, rec_sem, table_sem, halo_sem):
    tables = [
        pltpu.make_async_copy(source, target, table_sem.at[i])
        for i, (source, target) in enumerate(
            [(main_hbm, main), (tail_hbm, tail), (spread_hbm, spread), (lag_hbm, lag)])
    ]

    def piece(i):
        at = pl.ds(pl.multiple_of(i * 2 * HALF, 2 * HALF), 2 * HALF)
        return pltpu.make_async_copy(record_ref.at[:, at], rec.at[:, at], rec_sem.at[i])

    piece(0).start()
    tables[0].start()
    tables[1].start()
    for i in range(1, FRAMES // 2):
        piece(i).start()
    tables[2].start()
    tables[3].start()

    me = lax.axis_index("blk")
    count = lax.axis_size("blk")
    ahead = lax.rem(me + 2, count)
    behind = lax.rem(me + count - 2, count)
    parity = lax.rem(me, 2)
    beside = me + 1 - 2 * parity
    column = lax.div(me, 2)
    x, z = lax.div(column, 4), lax.rem(column, 4)
    columns = lax.div(count, 2)
    below = 2 * (x * 4 + lax.rem(z + 3, 4)) + parity
    above = 2 * (x * 4 + lax.rem(z + 1, 4)) + parity
    target = 2 * lax.rem(x * 4 + lax.rem(z + 2, 4) + 1, columns) + parity
    origin = lax.rem(column + columns - 1, columns)
    source_of_me = 2 * (lax.div(origin, 4) * 4 + lax.rem(lax.rem(origin, 4) + 2, 4)) + parity
    segment = lax.axis_index("pre")
    segments = lax.axis_size("pre")
    sooner = lax.rem(segment + segments - 1, segments)
    later = lax.rem(segment + 1, segments)
    barrier = pltpu.get_barrier_semaphore()
    for other in (ahead, behind, beside, below, above, target, source_of_me):
        pl.semaphore_signal(barrier, inc=1, device_id={"blk": other}, device_id_type=pl.DeviceIdType.MESH)
    for other in (sooner, later):
        pl.semaphore_signal(barrier, inc=1, device_id={"pre": other}, device_id_type=pl.DeviceIdType.MESH)
    pl.semaphore_wait(barrier, 9)

    halo = pltpu.make_async_remote_copy(
        src_ref=record_ref.at[:, pl.ds(0, HALO)],
        dst_ref=rec.at[:, pl.ds(LENGTH, HALO)],
        send_sem=halo_sem.at[0],
        recv_sem=halo_sem.at[1],
        device_id={"pre": sooner},
        device_id_type=pl.DeviceIdType.MESH,
    )

    @pl.when(segment > 0)
    def _():
        halo.start()

    @pl.when(segment == segments - 1)
    def _():
        rec[:, LENGTH:] = jnp.zeros((CH, HALO), BF)

    devices = {"y": beside, "z": ahead, "d": below, "e": target}

    def view(buffer, side, chunk):
        half, which = divmod(chunk, 8)
        if buffer > 3:
            return (early, late)[half].at[buffer - 4, passing_place(side, chunk)]
        ref = white if buffer == 0 else got.at[buffer - 1]
        if half == 0:
            return ref.at[:, pl.ds(which * 16, 16), :]
        return ref.at[pl.ds(which * 4, 4), pl.ds(128, 128), :]

    def copy(side, chunk, buffer, way, there):
        slot = sends_of(side, chunk).index((buffer, way, there))
        return pltpu.make_async_remote_copy(
            src_ref=view(buffer, side, chunk),
            dst_ref=view(there, side, chunk),
            send_sem=send_sem.at[slot, chunk],
            recv_sem=recv_sem.at[there - 1, chunk],
            device_id={"blk": devices[way]},
            device_id_type=pl.DeviceIdType.MESH,
        )

    def landed(side, chunk, buffer):
        return pltpu.make_async_remote_copy(
            src_ref=view(buffer, side, chunk),
            dst_ref=view(buffer, side, chunk),
            send_sem=send_sem.at[0, chunk],
            recv_sem=recv_sem.at[buffer - 1, chunk],
            device_id={"blk": beside},
            device_id_type=pl.DeviceIdType.MESH,
        )

    def on(condition):
        return lambda body: pl.when(condition)(body)

    def offer(side, chunk):
        for way, there in OWN[side][KINDS[chunk]]:
            copy(side, chunk, 0, way, there).start()

    def each_side(body):
        for side in range(2):
            @on(parity == side)
            def _():
                body(side)

    def visit(piece_at, step, steps):
        def body(side):
            for i in range(steps):
                if ARRIVALS[side][piece_at + i]:
                    @on(step == i)
                    def _():
                        for buffer, chunk in ARRIVALS[side][piece_at + i]:
                            landed(side, chunk, buffer).wait_recv()
                            onward = ONWARD[side][KINDS[chunk]].get(buffer)
                            if onward:
                                copy(side, chunk, buffer, *onward).start()

        each_side(body)

    def transform(raw, after):
        both = lax.dot_general(main[...], raw, NT, preferred_element_type=F32)
        ends = jnp.concatenate([after, after], 1)
        return (both[:ROWS] + both[ROWS:]) + lax.dot_general(
            tail[...], ends, NT, preferred_element_type=F32)

    piece(0).wait()
    tables[0].wait()
    tables[1].wait()
    held[...] = transform(rec[:, :HALF], rec[:, HALF : HALF + 128]).reshape(GROUPS + 2, 8, CH)
    keep = quality_ref[...].astype(F32).reshape(1, 1, CH)

    def frames(step):
        start = pl.multiple_of(step * 2 * HALF + HALF, HALF)
        one = pl.ds(start, HALF)
        two = pl.ds(pl.multiple_of(start + HALF, HALF), HALF)
        raw = jnp.concatenate([rec[:, one], rec[:, two]], 0)
        after = jnp.concatenate([
            rec[:, pl.ds(pl.multiple_of(start + HALF, HALF), 128)],
            rec[:, pl.ds(pl.multiple_of(start + 2 * HALF, HALF), 128)]], 0)
        pair = transform(raw, after)
        zero = held[...]
        first = pair[:, :CH].reshape(GROUPS + 2, 8, CH)
        second = pair[:, CH:].reshape(GROUPS + 2, 8, CH)
        held[...] = second
        group = lax.broadcasted_iota(jnp.int32, (GROUPS, 8, CH), 0)
        odd = (group % 2) == 1
        row = lax.broadcasted_iota(jnp.int32, (GROUPS, 8, CH), 1)

        def whiten(front, back):
            side = 0.25 * (front[:GROUPS] + front[2:])
            spec = 0.5 * front[1 : GROUPS + 1] - side
            other = 0.5 * back[1 : GROUPS + 1] + 0.25 * (back[:GROUPS] + back[2:])
            spec = spec + jnp.where(odd, -other, other)
            square = spec * spec
            level = jnp.sum(jnp.sum(square, 0), 0, keepdims=True).reshape(1, 1, CH) * (1.0 / FB)
            power = square + pltpu.roll(square, 4, 1)
            plain = spec * lax.rsqrt(power + (0.1 * level + 1e-06)) * keep
            swapped = pltpu.roll(plain, 4, 1)
            return plain, jnp.where(row < 4, swapped, -swapped)

        w0, t0 = whiten(zero, first)
        w1, t1 = whiten(first, second)
        at = pl.ds(pl.multiple_of(step * 16, 16), 16)
        white[:, at, :] = jnp.concatenate([w0, w1], 1).astype(BF)
        turned[:, at, :] = jnp.concatenate([t0, t1], 1).astype(BF)

    @pl.loop(0, FRAMES // 2)
    def _(step):
        visit(0, step, 16)

        @on(step < FRAMES // 2 - 1)
        def _():
            piece(step + 1).wait()

        @on(jnp.logical_and(step == FRAMES // 2 - 1, segment < segments - 1))
        def _():
            halo.wait_recv()

        frames(step)

        def body(side):
            for i in range(8):
                @on(step == i)
                def _():
                    offer(side, i)

        each_side(body)

    def rest(side):
        for chunk in range(8, CHUNKS):
            offer(side, chunk)

    each_side(rest)

    tables[2].wait()
    tables[3].wait()
    rows = lax.broadcasted_iota(jnp.int32, (PART * 8, 256), 0)
    cols = lax.broadcasted_iota(jnp.int32, (PART * 8, 256), 1)
    diagonal = (rows % 4) == (cols % 4)

    @pl.loop(0, GROUPS // 2)
    def _(step):
        visit(16, step, 16)
        for j in range(2):
            group = step * 2 + j
            own = jnp.concatenate([white[group], turned[group]], 1)
            for part in range(CH // PART):
                lines = pl.ds(part * PART * 8, PART * 8)
                table = lax.dot_general(spread[lines, :], own, NT, preferred_element_type=F32)
                left[group, lines, :] = jnp.where(diagonal, table, 0.0).astype(BF)

    def products(pair, one, two, store):
        for part in range(CH // PART):
            lines = pl.ds(part * PART * 8, PART * 8)
            pieces = []
            for j in range(2):
                group = 2 * pair + j
                right = jnp.concatenate([one[group], two[group]], 1)
                pieces.append(
                    jnp.dot(left[group, lines, :], right, preferred_element_type=F32).reshape(PART, 8, 2 * CH))
            store(part, jnp.concatenate(pieces, 1).astype(BF))

    def fill(which, one, two):
        @pl.loop(0, 2)
        def _(j):
            pair = which * 2 + j

            def store(part, value):
                far_ref[pl.ds(part * PART, PART), pl.ds(pl.multiple_of(pair * 16, 16), 16), :] = value

            products(pair, one, two, store)

    @pl.loop(0, 8)
    def _(which):
        visit(32, which, 8)
        fill(which, white, got.at[0])

    @pl.loop(0, 8)
    def _(which):
        visit(40, which, 8)
        lags(lag, far_ref, which, near_ref.at[which])

    @pl.loop(0, 8)
    def _(which):
        visit(48, which, 8)
        fill(which, got.at[1], got.at[2])

    visit(56, 0, 1)

    @on(segment > 0)
    def _():
        halo.wait_send()

    def sent(side):
        for chunk in range(CHUNKS):
            for buffer, way, there in sends_of(side, chunk):
                copy(side, chunk, buffer, way, there).wait_send()

    each_side(sent)


def exchange(record, quality):
    tables = [jnp.asarray(t) for t in half_tables() + (spread_table(), lag_table())]
    anywhere = pl.BlockSpec(memory_space=pl.ANY)
    return pl.pallas_call(
        exchange_kernel,
        out_shape=(
            pltpu.VMEM((CH // LAST, 2, NLAG, LAST, CH), F32),
            pltpu.VMEM((CH, 2 * FB, 2 * CH), BF),
        ),
        in_specs=[anywhere, pl.BlockSpec(memory_space=pltpu.VMEM)] + [anywhere] * 4,
        out_specs=(pl.BlockSpec(memory_space=pltpu.VMEM),) * 2,
        scratch_shapes=[
            pltpu.VMEM((CH, LENGTH + HALO), BF),
            pltpu.VMEM((2 * ROWS, HALF), BF),
            pltpu.VMEM((ROWS, 256), BF),
            pltpu.VMEM((CH * 8, 256), BF),
            pltpu.VMEM((NLAG, 2 * FB), BF),
            pltpu.VMEM((GROUPS + 2, 8, CH), F32),
            pltpu.VMEM((GROUPS, 256, CH), BF),
            pltpu.VMEM((GROUPS, 256, CH), BF),
            pltpu.VMEM((3, GROUPS, 256, CH), BF),
            pltpu.VMEM((2, 3, GROUPS, 16, CH), BF),
            pltpu.VMEM((2, 3, 4, 128, CH), BF),
            pltpu.VMEM((GROUPS, CH * 8, 256), BF),
            pltpu.SemaphoreType.DMA((6, CHUNKS)),
            pltpu.SemaphoreType.DMA((5, CHUNKS)),
            pltpu.SemaphoreType.DMA((FRAMES // 2,)),
            pltpu.SemaphoreType.DMA((4,)),
            pltpu.SemaphoreType.DMA((2,)),
        ],
        compiler_params=pltpu.CompilerParams(
            collective_id=0, has_side_effects=True, vmem_limit_bytes=39 * 2**20),
        name="exchange",
    )(record, quality.reshape(1, CH), *tables)


def last_kernel(lag, near, far, out_ref, staged, near_sem, far_sem):
    def store_near(which):
        at = pl.ds(pl.multiple_of(which * LAST, LAST), LAST)
        return pltpu.make_async_copy(near.at[which], out_ref.at[pl.ds(0, 2), :, at, :], near_sem.at[which])

    def store_far(which):
        at = pl.ds(pl.multiple_of(which * LAST, LAST), LAST)
        buffer = lax.rem(which, 2)
        return pltpu.make_async_copy(staged.at[buffer], out_ref.at[pl.ds(2, 2), :, at, :], far_sem.at[buffer])

    steps = CH // LAST

    @pl.loop(0, steps)
    def _(which):
        store_near(which).start()

        @pl.when(which > 1)
        def _():
            store_far(which - 2).wait()

        lags(lag, far, which, staged.at[lax.rem(which, 2)])
        store_far(which).start()

    for which in (steps - 2, steps - 1):
        store_far(which).wait()

    @pl.loop(0, steps)
    def _(which):
        store_near(which).wait()


def last(near, far):
    inside = pl.BlockSpec(memory_space=pltpu.VMEM)
    return pl.pallas_call(
        last_kernel,
        out_shape=jax.ShapeDtypeStruct((4, NLAG, CH, CH), F32),
        in_specs=[inside] * 3,
        out_specs=pl.BlockSpec(memory_space=pl.ANY),
        scratch_shapes=[
            pltpu.VMEM((2, 2, NLAG, LAST, CH), F32),
            pltpu.SemaphoreType.DMA((CH // LAST,)),
            pltpu.SemaphoreType.DMA((2,)),
        ],
        compiler_params=pltpu.CompilerParams(vmem_limit_bytes=8 * 2**20),
        name="last",
    )(jnp.asarray(lag_table()), near, far)


def shards(record, quality):
    return last(*exchange(record, quality))[None]


def solution(mesh):
    placed = (P("blk", "pre"), P("blk"))
    return jax.shard_map(
        shards,
        mesh=mesh,
        in_specs=placed,
        out_specs=P("pre", None, None, "blk", None),
        check_vma=False,
    )
```

```python
import math

import jax
import jax.numpy as jnp
import ml_dtypes
import numpy as np
from jax import lax
from jax.experimental import pallas as pl
from jax.experimental.pallas import tpu as pltpu
from jax.sharding import PartitionSpec as P

M = 512
R = 4
KT = 16
FB = 128
NLAG = 64
BAND0 = 16
CH = 128
HALF = 1024
FRAMES = 32
GROUPS = 32
ROWS = (GROUPS + 2) * 8
HALO = HALF + 128
NT = (((1,), (1,)), ((), ()))
BF = jnp.bfloat16
F32 = jnp.float32


def filter_taps():
    index = np.arange(KT, dtype=np.float32)
    centre = np.float32((KT - 1) / 2.0)
    shaped = np.sinc((index - centre) / np.float32(R)) * (
        0.54 - 0.46 * np.cos(2.0 * math.pi * index / (KT - 1))
    )
    return (shaped / np.sum(shaped)).astype(np.float32).astype(ml_dtypes.bfloat16)


def split(table):
    high = table.astype(np.float32).astype(ml_dtypes.bfloat16)
    low = (table - high.astype(np.float64)).astype(np.float32).astype(ml_dtypes.bfloat16)
    return high, low


def half_tables():
    taps = filter_taps().astype(np.float64)
    toeplitz = np.zeros((M // 2, HALF + 128))
    for m in range(M // 2):
        toeplitz[m, R * m : R * m + KT] = taps
    group = np.arange(-1, GROUPS + 1)
    bins = BAND0 + group[:, None] + 32 * np.arange(4)[None, :]
    phase = 2.0 * math.pi * ((bins[:, :, None] * np.arange(M // 2)) % M) / M
    both = np.stack([np.cos(phase), -np.sin(phase)], 1).reshape(ROWS, M // 2)
    table = both @ toeplitz
    high, low = split(table)
    main = np.concatenate([high[:, :HALF], low[:, :HALF]], 0)
    tail = np.concatenate([high[:, HALF:], low[:, HALF:]], 1)
    return main, tail


def lag_table():
    lags = np.arange(NLAG) - NLAG // 2
    bins = (BAND0 + np.arange(GROUPS)[:, None, None] + 32 * np.arange(4)[None, None, :])
    phase = 2.0 * math.pi * (((lags[:, None, None, None] + M) * bins[None]) % M) / M
    both = np.concatenate([np.cos(phase), -np.sin(phase)], 2).reshape(NLAG, 2 * FB)
    rounded = both.astype(np.float32).astype(ml_dtypes.bfloat16).astype(np.float32)
    return (rounded / 64.0).astype(ml_dtypes.bfloat16)


def spread_table():
    table = np.zeros((CH, 2, 4, 2, CH), np.float32)
    for c in range(CH):
        for o in range(2):
            table[c, o, :, o, c] = 1.0
    return table.reshape(CH * 8, 2 * CH).astype(ml_dtypes.bfloat16)


CHUNKS = 16
PART = 32
LENGTH = FRAMES * HALF
LAST = 16
BUFFERS = 4


KINDS = [5, 6, 6, 2, 2, 6, 3, 7, 7, 4, 2, 4, 5, 3, 7, 5]
OWN = {
    0: {2: [("y", 1), ("z", 2)], 3: [("y", 1)], 4: [("y", 1)], 5: [("d", 4), ("y", 1)],
        6: [("y", 1), ("z", 2)], 7: [("d", 4), ("y", 1)]},
    1: {kind: [("z", 2)] for kind in range(2, 8)},
}
ONWARD = {
    0: {
        2: {1: ("z", 3), 2: ("y", 3)},
        3: {1: ("z", 3)},
        4: {1: ("z", 3)},
        5: {1: ("z", 3), 2: ("y", 3), 4: ("d", 5), 5: ("e", 2)},
        6: {1: ("z", 3)},
        7: {1: ("z", 3), 4: ("d", 5), 5: ("e", 2)},
    },
    1: {
        2: {2: ("y", 1)},
        3: {2: ("y", 1), 1: ("z", 3), 3: ("y", 2)},
        4: {2: ("y", 1), 1: ("d", 4), 4: ("d", 5), 5: ("e", 3), 3: ("y", 2)},
        5: {2: ("y", 1)},
        6: {2: ("y", 1), 1: ("d", 4), 4: ("d", 5), 5: ("e", 3)},
        7: {2: ("y", 1), 1: ("z", 3)},
    },
}
ARRIVALS = (
    [
        [],
        [],
        [],
        [],
        [],
        [],
        [(4, 0)],
        [(2, 1)],
        [],
        [],
        [(2, 2)],
        [(5, 0), (1, 0)],
        [],
        [(2, 3)],
        [(4, 7)],
        [(1, 1)],
        [(2, 4), (2, 0), (1, 2)],
        [],
        [(2, 5)],
        [(5, 7), (1, 3)],
        [(3, 0)],
        [(4, 8)],
        [(1, 4)],
        [(3, 1)],
        [(4, 12)],
        [(1, 5)],
        [(2, 10)],
        [(4, 14), (1, 6)],
        [(3, 2)],
        [(4, 15)],
        [(1, 7)],
        [(3, 3)],
        [(2, 7)],
        [(1, 8)],
        [(3, 4)],
        [],
        [(5, 8)],
        [],
        [(1, 9)],
        [(3, 5)],
        [],
        [(5, 12)],
        [(1, 10), (3, 6)],
        [(5, 14), (1, 11)],
        [(3, 7), (5, 15), (1, 12)],
        [(3, 8), (2, 8), (1, 13)],
        [(3, 9), (2, 12), (1, 14)],
        [(3, 10), (2, 14), (1, 15)],
        [(3, 11)],
        [],
        [(2, 15)],
        [],
        [(2, 6)],
        [(3, 12)],
        [],
        [],
        [],
        [(2, 9), (3, 13)],
        [],
        [(2, 11)],
        [(3, 14)],
        [(2, 13)],
        [(3, 15)],
        [],
        [],
    ],
    [
        [],
        [],
        [],
        [],
        [],
        [],
        [(1, 0), (2, 0)],
        [],
        [],
        [(1, 1), (2, 1)],
        [],
        [],
        [(1, 2), (2, 2)],
        [],
        [],
        [(4, 1), (1, 3), (2, 3)],
        [(4, 2)],
        [(1, 4), (2, 4)],
        [],
        [(5, 1), (1, 5), (2, 5)],
        [],
        [],
        [(5, 2), (1, 6), (2, 6)],
        [],
        [(3, 1)],
        [(1, 7), (2, 7)],
        [],
        [(4, 5), (2, 8), (3, 3)],
        [],
        [(3, 2)],
        [(1, 8), (2, 9)],
        [],
        [(5, 5)],
        [(1, 9), (2, 10)],
        [],
        [],
        [],
        [],
        [(1, 10), (2, 11)],
        [],
        [],
        [(3, 5)],
        [(1, 11), (2, 12)],
        [(4, 9)],
        [(1, 12), (2, 13)],
        [(4, 11), (1, 13), (2, 14)],
        [(5, 9), (1, 14), (2, 15)],
        [(5, 11), (1, 15), (3, 6)],
        [],
        [],
        [],
        [],
        [(3, 9), (3, 4), (3, 7)],
        [],
        [],
        [],
        [(3, 11), (3, 0), (3, 8)],
        [],
        [(3, 10), (3, 13)],
        [],
        [(3, 12), (3, 14)],
        [],
        [],
        [(3, 15)],
        [],
    ],
)
PASSING = {0: (5, 7), 1: (4, 6)}


def sends_of(parity, chunk):
    kind = KINDS[chunk]
    return [(0,) + way for way in OWN[parity][kind]] + [
        (buffer,) + way for buffer, way in sorted(ONWARD[parity][kind].items())]


def passing_place(parity, chunk):
    first = chunk - chunk % 8
    return sum(KINDS[c] in PASSING[parity] for c in range(first, chunk))


def lags(lag, cross, which, target, rounds):
    lanes = pl.ds(rounds[0] * CH, len(rounds) * CH)
    for j in range(LAST):
        result = jnp.dot(lag[...], cross[which * LAST + j, :, lanes], preferred_element_type=F32)
        for i, d in enumerate(rounds):
            flat = target.at[d].reshape(NLAG * LAST, CH)
            flat[pl.ds(j, NLAG, stride=LAST), :] = result[:, i * CH : (i + 1) * CH]


def exchange_kernel(record_ref, quality_ref, main_hbm, tail_hbm, spread_hbm, lag_hbm, near_ref, far_ref,
                    rec, main, tail, spread, lag, held, white, turned, got, early, late, left,
                    send_sem, recv_sem, rec_sem, table_sem, halo_sem):
    tables = [
        pltpu.make_async_copy(source, target, table_sem.at[i])
        for i, (source, target) in enumerate(
            [(main_hbm, main), (tail_hbm, tail), (spread_hbm, spread), (lag_hbm, lag)])
    ]

    def piece(i):
        at = pl.ds(pl.multiple_of(i * 2 * HALF, 2 * HALF), 2 * HALF)
        return pltpu.make_async_copy(record_ref.at[:, at], rec.at[:, at], rec_sem.at[i])

    piece(0).start()
    tables[0].start()
    tables[1].start()
    for i in range(1, FRAMES // 2):
        piece(i).start()
    tables[2].start()
    tables[3].start()

    me = lax.axis_index("blk")
    count = lax.axis_size("blk")
    ahead = lax.rem(me + 2, count)
    behind = lax.rem(me + count - 2, count)
    parity = lax.rem(me, 2)
    beside = me + 1 - 2 * parity
    column = lax.div(me, 2)
    x, z = lax.div(column, 4), lax.rem(column, 4)
    columns = lax.div(count, 2)
    below = 2 * (x * 4 + lax.rem(z + 3, 4)) + parity
    above = 2 * (x * 4 + lax.rem(z + 1, 4)) + parity
    target = 2 * lax.rem(x * 4 + lax.rem(z + 2, 4) + 1, columns) + parity
    origin = lax.rem(column + columns - 1, columns)
    source_of_me = 2 * (lax.div(origin, 4) * 4 + lax.rem(lax.rem(origin, 4) + 2, 4)) + parity
    segment = lax.axis_index("pre")
    segments = lax.axis_size("pre")
    sooner = lax.rem(segment + segments - 1, segments)
    later = lax.rem(segment + 1, segments)
    barrier = pltpu.get_barrier_semaphore()
    for other in (ahead, behind, beside, below, above, target, source_of_me):
        pl.semaphore_signal(barrier, inc=1, device_id={"blk": other}, device_id_type=pl.DeviceIdType.MESH)
    for other in (sooner, later):
        pl.semaphore_signal(barrier, inc=1, device_id={"pre": other}, device_id_type=pl.DeviceIdType.MESH)
    pl.semaphore_wait(barrier, 9)

    halo = pltpu.make_async_remote_copy(
        src_ref=record_ref.at[:, pl.ds(0, HALO)],
        dst_ref=rec.at[:, pl.ds(LENGTH, HALO)],
        send_sem=halo_sem.at[0],
        recv_sem=halo_sem.at[1],
        device_id={"pre": sooner},
        device_id_type=pl.DeviceIdType.MESH,
    )

    @pl.when(segment > 0)
    def _():
        halo.start()

    @pl.when(segment == segments - 1)
    def _():
        rec[:, LENGTH:] = jnp.zeros((CH, HALO), BF)

    devices = {"y": beside, "z": ahead, "d": below, "e": target}

    def view(buffer, side, chunk):
        half, which = divmod(chunk, 8)
        if buffer > 3:
            return (early, late)[half].at[buffer - 4, passing_place(side, chunk)]
        ref = white if buffer == 0 else got.at[buffer - 1]
        if half == 0:
            return ref.at[:, pl.ds(which * 16, 16), :]
        return ref.at[pl.ds(which * 4, 4), pl.ds(128, 128), :]

    def copy(side, chunk, buffer, way, there):
        slot = sends_of(side, chunk).index((buffer, way, there))
        return pltpu.make_async_remote_copy(
            src_ref=view(buffer, side, chunk),
            dst_ref=view(there, side, chunk),
            send_sem=send_sem.at[slot, chunk],
            recv_sem=recv_sem.at[there - 1, chunk],
            device_id={"blk": devices[way]},
            device_id_type=pl.DeviceIdType.MESH,
        )

    def landed(side, chunk, buffer):
        return pltpu.make_async_remote_copy(
            src_ref=view(buffer, side, chunk),
            dst_ref=view(buffer, side, chunk),
            send_sem=send_sem.at[0, chunk],
            recv_sem=recv_sem.at[buffer - 1, chunk],
            device_id={"blk": beside},
            device_id_type=pl.DeviceIdType.MESH,
        )

    def on(condition):
        return lambda body: pl.when(condition)(body)

    def offer(side, chunk):
        for way, there in OWN[side][KINDS[chunk]]:
            copy(side, chunk, 0, way, there).start()

    def each_side(body):
        for side in range(2):
            @on(parity == side)
            def _():
                body(side)

    def visit(piece_at, step, steps):
        def body(side):
            for i in range(steps):
                if ARRIVALS[side][piece_at + i]:
                    @on(step == i)
                    def _():
                        for buffer, chunk in ARRIVALS[side][piece_at + i]:
                            landed(side, chunk, buffer).wait_recv()
                            onward = ONWARD[side][KINDS[chunk]].get(buffer)
                            if onward:
                                copy(side, chunk, buffer, *onward).start()

        each_side(body)

    def transform(raw, after):
        both = lax.dot_general(main[...], raw, NT, preferred_element_type=F32)
        ends = jnp.concatenate([after, after], 1)
        return (both[:ROWS] + both[ROWS:]) + lax.dot_general(
            tail[...], ends, NT, preferred_element_type=F32)

    piece(0).wait()
    tables[0].wait()
    tables[1].wait()
    held[...] = transform(rec[:, :HALF], rec[:, HALF : HALF + 128]).reshape(GROUPS + 2, 8, CH)
    keep = quality_ref[...].astype(F32).reshape(1, 1, CH)

    def frames(step):
        start = pl.multiple_of(step * 2 * HALF + HALF, HALF)
        one = pl.ds(start, HALF)
        two = pl.ds(pl.multiple_of(start + HALF, HALF), HALF)
        raw = jnp.concatenate([rec[:, one], rec[:, two]], 0)
        after = jnp.concatenate([
            rec[:, pl.ds(pl.multiple_of(start + HALF, HALF), 128)],
            rec[:, pl.ds(pl.multiple_of(start + 2 * HALF, HALF), 128)]], 0)
        pair = transform(raw, after)
        zero = held[...]
        first = pair[:, :CH].reshape(GROUPS + 2, 8, CH)
        second = pair[:, CH:].reshape(GROUPS + 2, 8, CH)
        held[...] = second
        group = lax.broadcasted_iota(jnp.int32, (GROUPS, 8, CH), 0)
        odd = (group % 2) == 1
        row = lax.broadcasted_iota(jnp.int32, (GROUPS, 8, CH), 1)

        def whiten(front, back):
            side = 0.25 * (front[:GROUPS] + front[2:])
            spec = 0.5 * front[1 : GROUPS + 1] - side
            other = 0.5 * back[1 : GROUPS + 1] + 0.25 * (back[:GROUPS] + back[2:])
            spec = spec + jnp.where(odd, -other, other)
            square = spec * spec
            level = jnp.sum(jnp.sum(square, 0), 0, keepdims=True).reshape(1, 1, CH) * (1.0 / FB)
            power = square + pltpu.roll(square, 4, 1)
            plain = spec * lax.rsqrt(power + (0.1 * level + 1e-06)) * keep
            swapped = pltpu.roll(plain, 4, 1)
            return plain, jnp.where(row < 4, swapped, -swapped)

        w0, t0 = whiten(zero, first)
        w1, t1 = whiten(first, second)
        at = pl.ds(pl.multiple_of(step * 16, 16), 16)
        white[:, at, :] = jnp.concatenate([w0, w1], 1).astype(BF)
        turned[:, at, :] = jnp.concatenate([t0, t1], 1).astype(BF)

    @pl.loop(0, FRAMES // 2)
    def _(step):
        visit(0, step, 16)

        @on(step < FRAMES // 2 - 1)
        def _():
            piece(step + 1).wait()

        @on(jnp.logical_and(step == FRAMES // 2 - 1, segment < segments - 1))
        def _():
            halo.wait_recv()

        frames(step)

        def body(side):
            for i in range(8):
                @on(step == i)
                def _():
                    offer(side, i)

        each_side(body)

    def rest(side):
        for chunk in range(8, CHUNKS):
            offer(side, chunk)

    each_side(rest)

    tables[2].wait()
    tables[3].wait()
    rows = lax.broadcasted_iota(jnp.int32, (PART * 8, 256), 0)
    cols = lax.broadcasted_iota(jnp.int32, (PART * 8, 256), 1)
    diagonal = (rows % 4) == (cols % 4)

    def fill(pair, table_of, rights, lanes):
        for part in range(CH // PART):
            lines = pl.ds(part * PART * 8, PART * 8)
            pieces = []
            for j in range(2):
                group = 2 * pair + j
                right = jnp.concatenate([ref[group] for ref in rights], 1)
                pieces.append(
                    jnp.dot(table_of(group, lines), right, preferred_element_type=F32).reshape(
                        PART, 8, len(rights) * CH))
            far_ref[pl.ds(part * PART, PART), pl.ds(pl.multiple_of(pair * 16, 16), 16), lanes] = (
                jnp.concatenate(pieces, 1).astype(BF))

    def make_table(group, lines):
        own = jnp.concatenate([white[group], turned[group]], 1)
        table = lax.dot_general(spread[lines, :], own, NT, preferred_element_type=F32)
        table = jnp.where(diagonal, table, 0.0).astype(BF)
        left[group, lines, :] = table
        return table

    def load_table(group, lines):
        return left[group, lines, :]

    @pl.loop(0, GROUPS // 2)
    def _(step):
        visit(16, step, 16)
        fill(step, make_table, [white], pl.ds(0, CH))

    @pl.loop(0, 8)
    def _(which):
        visit(32, which, 8)
        lags(lag, far_ref, which, near_ref.at[which], (0,))

    @pl.loop(0, 8)
    def _(which):
        visit(40, which, 8)

        @pl.loop(0, 2)
        def _(j):
            fill(which * 2 + j, load_table, [got.at[0]], pl.ds(CH, CH))

    @pl.loop(0, 8)
    def _(which):
        visit(48, which, 8)
        lags(lag, far_ref, which, near_ref.at[which], (1,))

    @pl.loop(0, 8)
    def _(which):
        visit(56, which, 8)

        @pl.loop(0, 2)
        def _(j):
            fill(which * 2 + j, load_table, [got.at[1], got.at[2]], pl.ds(0, 2 * CH))

    visit(64, 0, 1)

    @on(segment > 0)
    def _():
        halo.wait_send()

    def sent(side):
        for chunk in range(CHUNKS):
            for buffer, way, there in sends_of(side, chunk):
                copy(side, chunk, buffer, way, there).wait_send()

    each_side(sent)


def exchange(record, quality):
    tables = [jnp.asarray(t) for t in half_tables() + (spread_table(), lag_table())]
    anywhere = pl.BlockSpec(memory_space=pl.ANY)
    return pl.pallas_call(
        exchange_kernel,
        out_shape=(
            pltpu.VMEM((CH // LAST, 2, NLAG, LAST, CH), F32),
            pltpu.VMEM((CH, 2 * FB, 2 * CH), BF),
        ),
        in_specs=[anywhere, pl.BlockSpec(memory_space=pltpu.VMEM)] + [anywhere] * 4,
        out_specs=(pl.BlockSpec(memory_space=pltpu.VMEM),) * 2,
        scratch_shapes=[
            pltpu.VMEM((CH, LENGTH + HALO), BF),
            pltpu.VMEM((2 * ROWS, HALF), BF),
            pltpu.VMEM((ROWS, 256), BF),
            pltpu.VMEM((CH * 8, 256), BF),
            pltpu.VMEM((NLAG, 2 * FB), BF),
            pltpu.VMEM((GROUPS + 2, 8, CH), F32),
            pltpu.VMEM((GROUPS, 256, CH), BF),
            pltpu.VMEM((GROUPS, 256, CH), BF),
            pltpu.VMEM((3, GROUPS, 256, CH), BF),
            pltpu.VMEM((2, 4, GROUPS, 16, CH), BF),
            pltpu.VMEM((2, 4, 4, 128, CH), BF),
            pltpu.VMEM((GROUPS, CH * 8, 256), BF),
            pltpu.SemaphoreType.DMA((6, CHUNKS)),
            pltpu.SemaphoreType.DMA((5, CHUNKS)),
            pltpu.SemaphoreType.DMA((FRAMES // 2,)),
            pltpu.SemaphoreType.DMA((4,)),
            pltpu.SemaphoreType.DMA((2,)),
        ],
        compiler_params=pltpu.CompilerParams(
            collective_id=0, has_side_effects=True, vmem_limit_bytes=39 * 2**20),
        name="exchange",
    )(record, quality.reshape(1, CH), *tables)


def last_kernel(lag, near, far, out_ref, staged, near_sem, far_sem):
    def store_near(which):
        at = pl.ds(pl.multiple_of(which * LAST, LAST), LAST)
        return pltpu.make_async_copy(near.at[which], out_ref.at[pl.ds(0, 2), :, at, :], near_sem.at[which])

    def store_far(which):
        at = pl.ds(pl.multiple_of(which * LAST, LAST), LAST)
        buffer = lax.rem(which, BUFFERS)
        return pltpu.make_async_copy(staged.at[buffer], out_ref.at[pl.ds(2, 2), :, at, :], far_sem.at[buffer])

    steps = CH // LAST

    @pl.loop(0, steps)
    def _(which):
        store_near(which).start()

        @pl.when(which >= BUFFERS)
        def _():
            store_far(which - BUFFERS).wait()

        lags(lag, far, which, staged.at[lax.rem(which, BUFFERS)], (0, 1))
        store_far(which).start()

    for which in range(steps - BUFFERS, steps):
        store_far(which).wait()

    @pl.loop(0, steps)
    def _(which):
        store_near(which).wait()


def last(near, far):
    inside = pl.BlockSpec(memory_space=pltpu.VMEM)
    return pl.pallas_call(
        last_kernel,
        out_shape=jax.ShapeDtypeStruct((4, NLAG, CH, CH), F32),
        in_specs=[inside] * 3,
        out_specs=pl.BlockSpec(memory_space=pl.ANY),
        scratch_shapes=[
            pltpu.VMEM((BUFFERS, 2, NLAG, LAST, CH), F32),
            pltpu.SemaphoreType.DMA((CH // LAST,)),
            pltpu.SemaphoreType.DMA((BUFFERS,)),
        ],
        compiler_params=pltpu.CompilerParams(vmem_limit_bytes=8 * 2**20),
        name="last",
    )(jnp.asarray(lag_table()), near, far)


def shards(record, quality):
    return last(*exchange(record, quality))[None]


def solution(mesh):
    placed = (P("blk", "pre"), P("blk"))
    return jax.shard_map(
        shards,
        mesh=mesh,
        in_specs=placed,
        out_specs=P("pre", None, None, "blk", None),
        check_vma=False,
    )
```

```python
import math

import jax
import jax.numpy as jnp
import ml_dtypes
import numpy as np
from jax import lax
from jax.experimental import pallas as pl
from jax.experimental.pallas import tpu as pltpu
from jax.sharding import PartitionSpec as P

M = 512
R = 4
KT = 16
FB = 128
NLAG = 64
BAND0 = 16
CH = 128
HALF = 1024
FRAMES = 32
GROUPS = 32
ROWS = (GROUPS + 2) * 8
HALO = HALF + 128
NT = (((1,), (1,)), ((), ()))
BF = jnp.bfloat16
F32 = jnp.float32


def filter_taps():
    index = np.arange(KT, dtype=np.float32)
    centre = np.float32((KT - 1) / 2.0)
    shaped = np.sinc((index - centre) / np.float32(R)) * (
        0.54 - 0.46 * np.cos(2.0 * math.pi * index / (KT - 1))
    )
    return (shaped / np.sum(shaped)).astype(np.float32).astype(ml_dtypes.bfloat16)


def split(table):
    high = table.astype(np.float32).astype(ml_dtypes.bfloat16)
    low = (table - high.astype(np.float64)).astype(np.float32).astype(ml_dtypes.bfloat16)
    return high, low


def half_tables():
    taps = filter_taps().astype(np.float64)
    toeplitz = np.zeros((M // 2, HALF + 128))
    for m in range(M // 2):
        toeplitz[m, R * m : R * m + KT] = taps
    group = np.arange(-1, GROUPS + 1)
    bins = BAND0 + group[:, None] + 32 * np.arange(4)[None, :]
    phase = 2.0 * math.pi * ((bins[:, :, None] * np.arange(M // 2)) % M) / M
    both = np.stack([np.cos(phase), -np.sin(phase)], 1).reshape(ROWS, M // 2)
    table = both @ toeplitz
    high, low = split(table)
    main = np.concatenate([high[:, :HALF], low[:, :HALF]], 0)
    tail = np.concatenate([high[:, HALF:], low[:, HALF:]], 1)
    return main, tail


def lag_table():
    lags = np.arange(NLAG) - NLAG // 2
    bins = (BAND0 + np.arange(GROUPS)[:, None, None] + 32 * np.arange(4)[None, None, :])
    phase = 2.0 * math.pi * (((lags[:, None, None, None] + M) * bins[None]) % M) / M
    both = np.concatenate([np.cos(phase), -np.sin(phase)], 2).reshape(NLAG, 2 * FB)
    rounded = both.astype(np.float32).astype(ml_dtypes.bfloat16).astype(np.float32)
    return (rounded / 64.0).astype(ml_dtypes.bfloat16)


def spread_table():
    table = np.zeros((CH, 2, 4, 2, CH), np.float32)
    for c in range(CH):
        for o in range(2):
            table[c, o, :, o, c] = 1.0
    return table.reshape(CH * 8, 2 * CH).astype(ml_dtypes.bfloat16)


CHUNKS = 16
PART = 32
LENGTH = FRAMES * HALF
LAST = 16
BUFFERS = 4


KINDS = [5, 6, 6, 2, 2, 6, 3, 7, 7, 4, 2, 4, 5, 3, 7, 5]
OWN = {
    0: {2: [("y", 1), ("z", 2)], 3: [("y", 1)], 4: [("y", 1)], 5: [("d", 4), ("y", 1)],
        6: [("y", 1), ("z", 2)], 7: [("d", 4), ("y", 1)]},
    1: {kind: [("z", 2)] for kind in range(2, 8)},
}
ONWARD = {
    0: {
        2: {1: ("z", 3), 2: ("y", 3)},
        3: {1: ("z", 3)},
        4: {1: ("z", 3)},
        5: {1: ("z", 3), 2: ("y", 3), 4: ("d", 5), 5: ("e", 2)},
        6: {1: ("z", 3)},
        7: {1: ("z", 3), 4: ("d", 5), 5: ("e", 2)},
    },
    1: {
        2: {2: ("y", 1)},
        3: {2: ("y", 1), 1: ("z", 3), 3: ("y", 2)},
        4: {2: ("y", 1), 1: ("d", 4), 4: ("d", 5), 5: ("e", 3), 3: ("y", 2)},
        5: {2: ("y", 1)},
        6: {2: ("y", 1), 1: ("d", 4), 4: ("d", 5), 5: ("e", 3)},
        7: {2: ("y", 1), 1: ("z", 3)},
    },
}
ARRIVALS = (
    [
        [],
        [],
        [],
        [],
        [],
        [],
        [(4, 0)],
        [(2, 1)],
        [],
        [],
        [(2, 2)],
        [(5, 0), (1, 0)],
        [],
        [(2, 3)],
        [(4, 7)],
        [(1, 1)],
        [(2, 4), (2, 0), (1, 2)],
        [],
        [(2, 5)],
        [(5, 7), (1, 3)],
        [(3, 0)],
        [(4, 8)],
        [(1, 4)],
        [(3, 1)],
        [(4, 12)],
        [(1, 5)],
        [(2, 10)],
        [(4, 14), (1, 6)],
        [(3, 2)],
        [(4, 15)],
        [(1, 7)],
        [(3, 3)],
        [(2, 7)],
        [(1, 8)],
        [(3, 4)],
        [],
        [(5, 8)],
        [],
        [(1, 9)],
        [(3, 5)],
        [],
        [(5, 12)],
        [(1, 10), (3, 6)],
        [(5, 14), (1, 11)],
        [(3, 7), (5, 15), (1, 12)],
        [(3, 8), (2, 8), (1, 13)],
        [(3, 9), (2, 12), (1, 14)],
        [(3, 10), (2, 14), (1, 15)],
        [(3, 11)],
        [],
        [(2, 15)],
        [],
        [(2, 6)],
        [(3, 12)],
        [],
        [],
        [],
        [(2, 9), (3, 13)],
        [],
        [(2, 11)],
        [(3, 14)],
        [(2, 13)],
        [(3, 15)],
        [],
        [],
    ],
    [
        [],
        [],
        [],
        [],
        [],
        [],
        [(1, 0), (2, 0)],
        [],
        [],
        [(1, 1), (2, 1)],
        [],
        [],
        [(1, 2), (2, 2)],
        [],
        [],
        [(4, 1), (1, 3), (2, 3)],
        [(4, 2)],
        [(1, 4), (2, 4)],
        [],
        [(5, 1), (1, 5), (2, 5)],
        [],
        [],
        [(5, 2), (1, 6), (2, 6)],
        [],
        [(3, 1)],
        [(1, 7), (2, 7)],
        [],
        [(4, 5), (2, 8), (3, 3)],
        [],
        [(3, 2)],
        [(1, 8), (2, 9)],
        [],
        [(5, 5)],
        [(1, 9), (2, 10)],
        [],
        [],
        [],
        [],
        [(1, 10), (2, 11)],
        [],
        [],
        [(3, 5)],
        [(1, 11), (2, 12)],
        [(4, 9)],
        [(1, 12), (2, 13)],
        [(4, 11), (1, 13), (2, 14)],
        [(5, 9), (1, 14), (2, 15)],
        [(5, 11), (1, 15), (3, 6)],
        [],
        [],
        [],
        [],
        [(3, 9), (3, 4), (3, 7)],
        [],
        [],
        [],
        [(3, 11), (3, 0), (3, 8)],
        [],
        [(3, 10), (3, 13)],
        [],
        [(3, 12), (3, 14)],
        [],
        [],
        [(3, 15)],
        [],
    ],
)
PASSING = {0: (5, 7), 1: (4, 6)}


def sends_of(parity, chunk):
    kind = KINDS[chunk]
    return [(0,) + way for way in OWN[parity][kind]] + [
        (buffer,) + way for buffer, way in sorted(ONWARD[parity][kind].items())]


def passing_place(parity, chunk):
    first = chunk - chunk % 8
    return sum(KINDS[c] in PASSING[parity] for c in range(first, chunk))


def lags(lag, cross, which, target, rounds):
    lanes = pl.ds(rounds[0] * CH, len(rounds) * CH)
    for j in range(LAST):
        result = jnp.dot(lag[...], cross[which * LAST + j, :, lanes], preferred_element_type=F32)
        for i, d in enumerate(rounds):
            flat = target.at[d].reshape(NLAG * LAST, CH)
            flat[pl.ds(j, NLAG, stride=LAST), :] = result[:, i * CH : (i + 1) * CH]


def exchange_kernel(record_ref, quality_ref, main_hbm, tail_hbm, spread_hbm, lag_hbm, near_ref, far_ref,
                    rec, main, tail, spread, lag, held, white, turned, got, early, late, left,
                    send_sem, recv_sem, rec_sem, table_sem, halo_sem):
    tables = [
        pltpu.make_async_copy(source, target, table_sem.at[i])
        for i, (source, target) in enumerate(
            [(main_hbm, main), (tail_hbm, tail), (spread_hbm, spread), (lag_hbm, lag)])
    ]

    def piece(i):
        at = pl.ds(pl.multiple_of(i * 2 * HALF, 2 * HALF), 2 * HALF)
        return pltpu.make_async_copy(record_ref.at[:, at], rec.at[:, at], rec_sem.at[i])

    piece(0).start()
    tables[0].start()
    tables[1].start()
    piece(1).start()

    me = lax.axis_index("blk")
    count = lax.axis_size("blk")
    ahead = lax.rem(me + 2, count)
    behind = lax.rem(me + count - 2, count)
    parity = lax.rem(me, 2)
    beside = me + 1 - 2 * parity
    column = lax.div(me, 2)
    x, z = lax.div(column, 4), lax.rem(column, 4)
    columns = lax.div(count, 2)
    below = 2 * (x * 4 + lax.rem(z + 3, 4)) + parity
    above = 2 * (x * 4 + lax.rem(z + 1, 4)) + parity
    target = 2 * lax.rem(x * 4 + lax.rem(z + 2, 4) + 1, columns) + parity
    origin = lax.rem(column + columns - 1, columns)
    source_of_me = 2 * (lax.div(origin, 4) * 4 + lax.rem(lax.rem(origin, 4) + 2, 4)) + parity
    segment = lax.axis_index("pre")
    segments = lax.axis_size("pre")
    sooner = lax.rem(segment + segments - 1, segments)
    later = lax.rem(segment + 1, segments)
    barrier = pltpu.get_barrier_semaphore()
    for other in (ahead, behind, beside, below, above, target, source_of_me):
        pl.semaphore_signal(barrier, inc=1, device_id={"blk": other}, device_id_type=pl.DeviceIdType.MESH)
    for other in (sooner, later):
        pl.semaphore_signal(barrier, inc=1, device_id={"pre": other}, device_id_type=pl.DeviceIdType.MESH)
    pl.semaphore_wait(barrier, 9)

    halo = pltpu.make_async_remote_copy(
        src_ref=record_ref.at[:, pl.ds(0, HALO)],
        dst_ref=rec.at[:, pl.ds(LENGTH, HALO)],
        send_sem=halo_sem.at[0],
        recv_sem=halo_sem.at[1],
        device_id={"pre": sooner},
        device_id_type=pl.DeviceIdType.MESH,
    )

    @pl.when(segment > 0)
    def _():
        halo.start()

    @pl.when(segment == segments - 1)
    def _():
        rec[:, LENGTH:] = jnp.zeros((CH, HALO), BF)

    devices = {"y": beside, "z": ahead, "d": below, "e": target}

    def view(buffer, side, chunk):
        half, which = divmod(chunk, 8)
        if buffer > 3:
            return (early, late)[half].at[buffer - 4, passing_place(side, chunk)]
        ref = white if buffer == 0 else got.at[buffer - 1]
        if half == 0:
            return ref.at[:, pl.ds(which * 16, 16), :]
        return ref.at[pl.ds(which * 4, 4), pl.ds(128, 128), :]

    def copy(side, chunk, buffer, way, there):
        slot = sends_of(side, chunk).index((buffer, way, there))
        return pltpu.make_async_remote_copy(
            src_ref=view(buffer, side, chunk),
            dst_ref=view(there, side, chunk),
            send_sem=send_sem.at[slot, chunk],
            recv_sem=recv_sem.at[there - 1, chunk],
            device_id={"blk": devices[way]},
            device_id_type=pl.DeviceIdType.MESH,
        )

    def landed(side, chunk, buffer):
        return pltpu.make_async_remote_copy(
            src_ref=view(buffer, side, chunk),
            dst_ref=view(buffer, side, chunk),
            send_sem=send_sem.at[0, chunk],
            recv_sem=recv_sem.at[buffer - 1, chunk],
            device_id={"blk": beside},
            device_id_type=pl.DeviceIdType.MESH,
        )

    def on(condition):
        return lambda body: pl.when(condition)(body)

    def offer(side, chunk):
        for way, there in OWN[side][KINDS[chunk]]:
            copy(side, chunk, 0, way, there).start()

    def each_side(body):
        for side in range(2):
            @on(parity == side)
            def _():
                body(side)

    def visit(piece_at, step, steps):
        def body(side):
            for i in range(steps):
                if ARRIVALS[side][piece_at + i]:
                    @on(step == i)
                    def _():
                        for buffer, chunk in ARRIVALS[side][piece_at + i]:
                            landed(side, chunk, buffer).wait_recv()
                            onward = ONWARD[side][KINDS[chunk]].get(buffer)
                            if onward:
                                copy(side, chunk, buffer, *onward).start()

        each_side(body)

    def transform(raw, after):
        both = lax.dot_general(main[...], raw, NT, preferred_element_type=F32)
        ends = jnp.concatenate([after, after], 1)
        return (both[:ROWS] + both[ROWS:]) + lax.dot_general(
            tail[...], ends, NT, preferred_element_type=F32)

    piece(0).wait()
    tables[0].wait()
    tables[1].wait()
    for i in range(2, FRAMES // 2):
        piece(i).start()
    tables[2].start()
    tables[3].start()
    held[...] = transform(rec[:, :HALF], rec[:, HALF : HALF + 128]).reshape(GROUPS + 2, 8, CH)
    keep = quality_ref[...].astype(F32).reshape(1, 1, CH)

    def frames(step):
        start = pl.multiple_of(step * 2 * HALF + HALF, HALF)
        one = pl.ds(start, HALF)
        two = pl.ds(pl.multiple_of(start + HALF, HALF), HALF)
        raw = jnp.concatenate([rec[:, one], rec[:, two]], 0)
        after = jnp.concatenate([
            rec[:, pl.ds(pl.multiple_of(start + HALF, HALF), 128)],
            rec[:, pl.ds(pl.multiple_of(start + 2 * HALF, HALF), 128)]], 0)
        pair = transform(raw, after)
        zero = held[...]
        first = pair[:, :CH].reshape(GROUPS + 2, 8, CH)
        second = pair[:, CH:].reshape(GROUPS + 2, 8, CH)
        held[...] = second
        group = lax.broadcasted_iota(jnp.int32, (GROUPS, 8, CH), 0)
        odd = (group % 2) == 1
        row = lax.broadcasted_iota(jnp.int32, (GROUPS, 8, CH), 1)

        def whiten(front, back):
            side = 0.25 * (front[:GROUPS] + front[2:])
            spec = 0.5 * front[1 : GROUPS + 1] - side
            other = 0.5 * back[1 : GROUPS + 1] + 0.25 * (back[:GROUPS] + back[2:])
            spec = spec + jnp.where(odd, -other, other)
            square = spec * spec
            level = jnp.sum(jnp.sum(square, 0), 0, keepdims=True).reshape(1, 1, CH) * (1.0 / FB)
            power = square + pltpu.roll(square, 4, 1)
            plain = spec * lax.rsqrt(power + (0.1 * level + 1e-06)) * keep
            swapped = pltpu.roll(plain, 4, 1)
            return plain, jnp.where(row < 4, swapped, -swapped)

        w0, t0 = whiten(zero, first)
        w1, t1 = whiten(first, second)
        at = pl.ds(pl.multiple_of(step * 16, 16), 16)
        white[:, at, :] = jnp.concatenate([w0, w1], 1).astype(BF)
        turned[:, at, :] = jnp.concatenate([t0, t1], 1).astype(BF)

    @pl.loop(0, FRAMES // 2)
    def _(step):
        visit(0, step, 16)

        @on(step < FRAMES // 2 - 1)
        def _():
            piece(step + 1).wait()

        @on(jnp.logical_and(step == FRAMES // 2 - 1, segment < segments - 1))
        def _():
            halo.wait_recv()

        frames(step)

        def body(side):
            for i in range(8):
                @on(step == i)
                def _():
                    offer(side, i)

        each_side(body)

    def rest(side):
        for chunk in range(8, CHUNKS):
            offer(side, chunk)

    each_side(rest)

    tables[2].wait()
    tables[3].wait()
    rows = lax.broadcasted_iota(jnp.int32, (PART * 8, 256), 0)
    cols = lax.broadcasted_iota(jnp.int32, (PART * 8, 256), 1)
    diagonal = (rows % 4) == (cols % 4)

    def fill(pair, table_of, rights, lanes):
        for part in range(CH // PART):
            lines = pl.ds(part * PART * 8, PART * 8)
            pieces = []
            for j in range(2):
                group = 2 * pair + j
                right = jnp.concatenate([ref[group] for ref in rights], 1)
                pieces.append(
                    jnp.dot(table_of(group, lines), right, preferred_element_type=F32).reshape(
                        PART, 8, len(rights) * CH))
            far_ref[pl.ds(part * PART, PART), pl.ds(pl.multiple_of(pair * 16, 16), 16), lanes] = (
                jnp.concatenate(pieces, 1).astype(BF))

    def make_table(group, lines):
        own = jnp.concatenate([white[group], turned[group]], 1)
        table = lax.dot_general(spread[lines, :], own, NT, preferred_element_type=F32)
        table = jnp.where(diagonal, table, 0.0).astype(BF)
        left[group, lines, :] = table
        return table

    def load_table(group, lines):
        return left[group, lines, :]

    @pl.loop(0, GROUPS // 2)
    def _(step):
        visit(16, step, 16)
        fill(step, make_table, [white], pl.ds(0, CH))

    @pl.loop(0, 8)
    def _(which):
        visit(32, which, 8)
        lags(lag, far_ref, which, near_ref.at[which], (0,))

    @pl.loop(0, 8)
    def _(which):
        visit(40, which, 8)

        @pl.loop(0, 2)
        def _(j):
            fill(which * 2 + j, load_table, [got.at[0]], pl.ds(CH, CH))

    @pl.loop(0, 8)
    def _(which):
        visit(48, which, 8)
        lags(lag, far_ref, which, near_ref.at[which], (1,))

    @pl.loop(0, 8)
    def _(which):
        visit(56, which, 8)

        @pl.loop(0, 2)
        def _(j):
            fill(which * 2 + j, load_table, [got.at[1], got.at[2]], pl.ds(0, 2 * CH))

    visit(64, 0, 1)

    @on(segment > 0)
    def _():
        halo.wait_send()

    def sent(side):
        for chunk in range(CHUNKS):
            for buffer, way, there in sends_of(side, chunk):
                copy(side, chunk, buffer, way, there).wait_send()

    each_side(sent)


def exchange(record, quality):
    tables = [jnp.asarray(t) for t in half_tables() + (spread_table(), lag_table())]
    anywhere = pl.BlockSpec(memory_space=pl.ANY)
    return pl.pallas_call(
        exchange_kernel,
        out_shape=(
            pltpu.VMEM((CH // LAST, 2, NLAG, LAST, CH), F32),
            pltpu.VMEM((CH, 2 * FB, 2 * CH), BF),
        ),
        in_specs=[anywhere, pl.BlockSpec(memory_space=pltpu.VMEM)] + [anywhere] * 4,
        out_specs=(pl.BlockSpec(memory_space=pltpu.VMEM),) * 2,
        scratch_shapes=[
            pltpu.VMEM((CH, LENGTH + HALO), BF),
            pltpu.VMEM((2 * ROWS, HALF), BF),
            pltpu.VMEM((ROWS, 256), BF),
            pltpu.VMEM((CH * 8, 256), BF),
            pltpu.VMEM((NLAG, 2 * FB), BF),
            pltpu.VMEM((GROUPS + 2, 8, CH), F32),
            pltpu.VMEM((GROUPS, 256, CH), BF),
            pltpu.VMEM((GROUPS, 256, CH), BF),
            pltpu.VMEM((3, GROUPS, 256, CH), BF),
            pltpu.VMEM((2, 4, GROUPS, 16, CH), BF),
            pltpu.VMEM((2, 4, 4, 128, CH), BF),
            pltpu.VMEM((GROUPS, CH * 8, 256), BF),
            pltpu.SemaphoreType.DMA((6, CHUNKS)),
            pltpu.SemaphoreType.DMA((5, CHUNKS)),
            pltpu.SemaphoreType.DMA((FRAMES // 2,)),
            pltpu.SemaphoreType.DMA((4,)),
            pltpu.SemaphoreType.DMA((2,)),
        ],
        compiler_params=pltpu.CompilerParams(
            collective_id=0, has_side_effects=True, vmem_limit_bytes=39 * 2**20),
        name="exchange",
    )(record, quality.reshape(1, CH), *tables)


def last_kernel(lag, near, far, out_ref, staged, near_sem, far_sem):
    def store_near(which):
        at = pl.ds(pl.multiple_of(which * LAST, LAST), LAST)
        return pltpu.make_async_copy(near.at[which], out_ref.at[pl.ds(0, 2), :, at, :], near_sem.at[which])

    def store_far(which):
        at = pl.ds(pl.multiple_of(which * LAST, LAST), LAST)
        buffer = lax.rem(which, BUFFERS)
        return pltpu.make_async_copy(staged.at[buffer], out_ref.at[pl.ds(2, 2), :, at, :], far_sem.at[buffer])

    steps = CH // LAST

    @pl.loop(0, steps)
    def _(which):
        store_near(which).start()

        @pl.when(which >= BUFFERS)
        def _():
            store_far(which - BUFFERS).wait()

        lags(lag, far, which, staged.at[lax.rem(which, BUFFERS)], (0, 1))
        store_far(which).start()

    for which in range(steps - BUFFERS, steps):
        store_far(which).wait()

    @pl.loop(0, steps)
    def _(which):
        store_near(which).wait()


def last(near, far):
    inside = pl.BlockSpec(memory_space=pltpu.VMEM)
    return pl.pallas_call(
        last_kernel,
        out_shape=jax.ShapeDtypeStruct((4, NLAG, CH, CH), F32),
        in_specs=[inside] * 3,
        out_specs=pl.BlockSpec(memory_space=pl.ANY),
        scratch_shapes=[
            pltpu.VMEM((BUFFERS, 2, NLAG, LAST, CH), F32),
            pltpu.SemaphoreType.DMA((CH // LAST,)),
            pltpu.SemaphoreType.DMA((BUFFERS,)),
        ],
        compiler_params=pltpu.CompilerParams(vmem_limit_bytes=8 * 2**20),
        name="last",
    )(jnp.asarray(lag_table()), near, far)


def shards(record, quality):
    return last(*exchange(record, quality))[None]


def solution(mesh):
    placed = (P("blk", "pre"), P("blk"))
    return jax.shard_map(
        shards,
        mesh=mesh,
        in_specs=placed,
        out_specs=P("pre", None, None, "blk", None),
        check_vma=False,
    )
```
